32 devices in a mesh: patch: 16 (over z, y, x), strip: 2 (over core).
Axes of the slice: x: 2, y: 2, z: 4, core: 2. Of those that a mesh axis runs over, the one named last changes fastest.
Arguments:
- features: float32 [32768, 128], P(('patch', 'strip')), may hold values from -6 to 6
- lap_tiles: float32 [512, 6, 4096], P(('patch', 'strip')), may hold values from -0.3125 to 0.3125
- columns: int32 [512, 6], P(('patch', 'strip')), may hold values from 0 to 511, as said below
- weights: float32 [3, 64, 64], replicated, may hold values from -0.75 to 0.75
- bias_term: float32 [64], replicated, may hold values from -4 to 4
- cotangent: float32 [32768, 128], P(('patch', 'strip')), may hold values from -6 to 6
Outputs:
- output: float32 [32768, 128], P(('patch', 'strip'))
- input_grad: float32 [32768, 128], P(('patch', 'strip'))
- weight_grad: float32 [3, 64, 64], replicated
- bias_grad: float32 [64], replicated
The draws below stay inside these ranges and needn't reach their ends.
Inputs may be any that keep to these rules, and one draw needn't show every extreme that they name: `columns`: entry 0 of a block's 6 entries is the block itself and entry 1 lies exactly 4 blocks before or after it; all entries of a block are distinct blocks within 4 of it in the cyclic order of the 512 blocks.
All inputs are finite; a program needn't handle non-finite values.
Results may differ from the reference program's by a relative error of at most 0.0001.
Values sent between devices are 32-bit elements; how exact they have to be, the bound alone decides.
A program may use at most 64 MiB of HBM per device.

```python
import math
import jax
import jax.numpy as jnp
from jax import lax

C = 64
BATCH = 2
PB = 64
NB = 6
HB = 4
BLK_DEV = 16
BLOCKS = 512
PIXELS = 32768


def draw_columns(key, part):
    block_ids = jnp.arange(BLOCKS, dtype=jnp.int32)
    sign_key = jax.random.fold_in(key, 11)
    rank_key = jax.random.fold_in(key, 12)
    sign_pick = jax.random.randint(sign_key, (BLOCKS,), 0, 2).astype(jnp.int32) * 2 - 1
    far_offset = sign_pick * HB
    candidates = jnp.concatenate([jnp.arange(-HB, 0), jnp.arange(1, HB + 1)]).astype(jnp.int32)
    scores = jax.random.randint(rank_key, (BLOCKS, 2 * HB), 0, 1 << 20).astype(jnp.int32) * (2 * HB) + jnp.arange(2 * HB, dtype=jnp.int32)
    scores = jnp.where(candidates[None, :] == far_offset[:, None], -1, scores)
    ranking = jnp.argsort(scores, axis=1)
    chosen = jnp.take_along_axis(jnp.broadcast_to(candidates, (BLOCKS, 2 * HB)), ranking, axis=1)[:, :NB - 1]
    offsets = jnp.concatenate([jnp.zeros((BLOCKS, 1), jnp.int32), chosen], axis=1)
    return jnp.mod(block_ids[:, None] + offsets, BLOCKS).astype(jnp.int32)


def shard_levels(rng, dims, cuts, least, high):
    loudness, own = 1.0, jax.random.fold_in(rng, 6)
    for axis_at, shards_of in cuts:
        heights = jnp.exp(jax.random.uniform(jax.random.fold_in(own, axis_at), (shards_of,), jnp.float32, least / len(cuts), high / len(cuts)))
        loudness = loudness * jnp.repeat(heights, dims[axis_at] // shards_of).reshape([-1 if axis == axis_at else 1 for axis in range(len(dims))])
    return loudness


def centred(rng, dims, width, limit, cuts=(), held_as=jnp.bfloat16):
    drawn = jax.random.normal(rng, dims, jnp.float32) * width
    if len(cuts) > 0:
        drawn = shard_levels(rng, dims, cuts, -0.22, 0.18) * drawn
    return jnp.clip(drawn, min=-limit, max=limit).astype(held_as)


def setup_inputs(seed: int = 0) -> dict:
    key_of = jax.random.split(jax.random.key(seed), 7)
    return {
        "features": centred(key_of[0], (PIXELS, BATCH * C), 1.0, 6.0, ((0, 32),), jnp.float32),
        "lap_tiles": centred(key_of[1], (BLOCKS, NB, PB * PB), (NB * PB) ** -0.5, 0.3125, ((0, 32),), jnp.float32),
        "columns": draw_columns(jax.random.fold_in(key_of[6], 71), 0),
        "weights": centred(key_of[3], (3, C, C), C ** -0.5, 0.75, (), jnp.float32),
        "bias_term": centred(key_of[4], (C,), 1.0, 4.0, (), jnp.float32),
        "cotangent": centred(key_of[5], (PIXELS, BATCH * C), 1.0, 6.0, ((0, 32),), jnp.float32),
    }


highest = lax.Precision.HIGHEST

def apply_lap(blocks, lap_tiles, columns):
    groups = blocks.shape[0] // BLK_DEV
    tile_groups = lap_tiles.reshape(groups, BLK_DEV, NB, PB, PB)
    column_groups = columns.reshape(groups, BLK_DEV, NB)

    def one_group(pieces):
        tile_part, column_part = pieces
        picked = blocks[column_part]
        return jnp.einsum('bjpq,bjqf->bpf', tile_part, picked, precision=highest)
    return lax.map(one_group, (tile_groups, column_groups)).reshape(blocks.shape)

def apply_lap_t(blocks, lap_tiles, columns):
    groups = blocks.shape[0] // BLK_DEV
    feat_width = blocks.shape[2]
    tile_groups = lap_tiles.reshape(groups, BLK_DEV, NB, PB, PB)
    column_groups = columns.reshape(groups, BLK_DEV, NB)
    vector_groups = blocks.reshape(groups, BLK_DEV, PB, feat_width)

    def one_group(total, pieces):
        tile_part, column_part, vector_part = pieces
        contrib = jnp.einsum('bjpq,bpf->bjqf', tile_part, vector_part, precision=highest)
        total = total.at[column_part.reshape(-1)].add(contrib.reshape(-1, PB, feat_width))
        return (total, None)
    total, unused = lax.scan(one_group, jnp.zeros_like(blocks), (tile_groups, column_groups, vector_groups))
    return total

def reference(features, lap_tiles, columns, weights, bias_term, cotangent):
    pixel_count, feat_width = features.shape
    block_count = pixel_count // PB
    zeroth = features.reshape(block_count, PB, feat_width)
    first_term = apply_lap(zeroth, lap_tiles, columns)
    second_term = 2.0 * apply_lap(first_term, lap_tiles, columns) - zeroth
    cheb_terms = (zeroth, first_term, second_term)
    mixed_sum = jnp.einsum('nbc,cd->nbd', zeroth.reshape(pixel_count, BATCH, C), weights[0], precision=highest)
    mixed_sum = mixed_sum + jnp.einsum('nbc,cd->nbd', first_term.reshape(pixel_count, BATCH, C), weights[1], precision=highest)
    mixed_sum = mixed_sum + jnp.einsum('nbc,cd->nbd', second_term.reshape(pixel_count, BATCH, C), weights[2], precision=highest)
    output = (mixed_sum + bias_term).reshape(pixel_count, feat_width)
    grad_maps = cotangent.reshape(pixel_count, BATCH, C)
    back_zero = jnp.einsum('nbd,cd->nbc', grad_maps, weights[0], precision=highest).reshape(block_count, PB, feat_width)
    back_one = jnp.einsum('nbd,cd->nbc', grad_maps, weights[1], precision=highest).reshape(block_count, PB, feat_width)
    back_two = jnp.einsum('nbd,cd->nbc', grad_maps, weights[2], precision=highest).reshape(block_count, PB, feat_width)
    inner_sum = back_one + 2.0 * apply_lap_t(back_two, lap_tiles, columns)
    input_grad = (back_zero - back_two + apply_lap_t(inner_sum, lap_tiles, columns)).reshape(pixel_count, feat_width)
    grad_scale = 1.0 / math.sqrt(BATCH * pixel_count)
    weight_grad = jnp.stack([jnp.einsum('nbc,nbd->cd', term_part.reshape(pixel_count, BATCH, C), grad_maps, precision=highest) for term_part in cheb_terms]) * grad_scale
    bias_grad = lax.optimization_barrier(jnp.sum(grad_maps, axis=(0, 1))) * grad_scale
    return (output, input_grad, weight_grad, bias_grad)
```

```python
import functools
import math

import jax
import jax.numpy as jnp
from jax import lax
from jax.experimental import pallas as pl
from jax.experimental.pallas import tpu as pltpu
from jax.sharding import PartitionSpec as P

MESH = pl.DeviceIdType.MESH
PEERS = 8
f32, bf16 = jnp.float32, jnp.bfloat16


def halves(x):
    hi = x.astype(bf16)
    return hi, (x - hi.astype(f32)).astype(bf16)


def dot(a, b):
    return jnp.dot(a, b, preferred_element_type=f32)


def side_by_side(x):
    return jnp.concatenate(halves(x), axis=1)


def stacked(x):
    return jnp.concatenate(halves(x), axis=0)


def both_maps(w):
    zero = jnp.zeros_like(w)
    return jnp.concatenate(
        [jnp.concatenate([w, zero], axis=1), jnp.concatenate([zero, w], axis=1)], axis=0
    )


def body(
    dims,
    f_hbm, lap_hbm, col, w_ref, b_ref, cot_hbm,
    out_hbm, ig_hbm, wg_ref, bg_ref,
    f_v, cot_v, lap_v, y, dhi, dlo, fc, tc, cc, uc, wf, wb, out_v, ig_v,
    f_in, t_in, u_in, v_in, t_out, u_out, v_out,
    grads, part_in, seg, cross, final,
    send, recv, a_send, a_recv, b_send, b_recv, c_send, c_recv, local, put,
):
    nb, pb, blocks, hb, total, scale = dims
    half, width = hb * pb, f_v.shape[1]
    rows = blocks * pb
    groups = blocks // hb
    chan = width // 2
    strips = lax.axis_size("strip")
    n = lax.axis_size("patch") * strips
    me = lax.axis_index("patch") * strips + lax.axis_index("strip")
    first = me * blocks
    teams = n // PEERS
    team, rank = me // PEERS, me % PEERS

    def at(index):
        return (index // strips, index % strips)

    prev, nxt = at((me + n - 1) % n), at((me + 1) % n)
    mates = [(rank + o) % PEERS for o in range(1, PEERS)]
    others = [(team + o) % teams for o in range(1, teams)]

    barrier = pltpu.get_barrier_semaphore()
    greeted = [prev, nxt]
    greeted += [at(team * PEERS + m) for m in mates]
    greeted += [at(t * PEERS + rank) for t in others]
    for device in greeted:
        pl.semaphore_signal(barrier, inc=1, device_id=device, device_id_type=MESH)
    load_lap = pltpu.make_async_copy(lap_hbm, lap_v, local.at[0])
    load_cot = pltpu.make_async_copy(cot_hbm, cot_v, local.at[1])
    load_f = pltpu.make_async_copy(f_hbm, f_v, local.at[2])
    load_lap.start()
    load_cot.start()
    load_f.start()
    pl.semaphore_wait(barrier, len(greeted))

    def swap(slot, to_next, to_prev, landing):
        pair = []
        for i, (src, device) in enumerate(((to_next, nxt), (to_prev, prev))):
            copy = pltpu.make_async_remote_copy(
                src_ref=src,
                dst_ref=landing.at[i],
                send_sem=send.at[2 * slot + i],
                recv_sem=recv.at[2 * slot + i],
                device_id=device,
                device_id_type=MESH,
            )
            copy.start()
            pair.append(copy)
        return pair

    f_swap = swap(0, f_hbm.at[pl.ds(rows - half, half)], f_hbm.at[pl.ds(0, half)], f_in)

    load_lap.wait()
    low = lax.broadcasted_iota(jnp.int32, (8, 128), 1) < pb

    def spread(j, carry):
        for eight in range(blocks // 8):
            for r in range(pb // 2):
                x = lap_v[j, pl.ds(8 * eight, 8), pl.ds(128 * r, 128)]
                turned = pltpu.roll(x, 64, 1)
                start = 8 * eight * nb * pb + j * pb + 2 * r
                y[pl.ds(start, 8, stride=nb * pb), :] = jnp.where(low, x, turned)
                y[pl.ds(start + 1, 8, stride=nb * pb), :] = jnp.where(low, turned, x)
        return carry

    lax.fori_loop(0, nb, spread, 0)

    side = lax.broadcasted_iota(jnp.int32, (pb, 128), 1) // pb

    def band(g, carry):
        for i in range(hb):
            b = g * hb + i
            spots = []
            for j in range(nb):
                d = col[j, b] - (first + b - hb)
                d = jnp.where(d < 0, d + total, d)
                d = jnp.where(d >= total, d - total, d)
                spots.append(d + i)
            own = pl.ds(pl.multiple_of(b * pb, pb), pb)
            for m in range(3 * hb // 2):
                columns = pl.ds(128 * m, 128)
                if 2 * m + 1 < i or 2 * m > i + 2 * hb:
                    dhi[own, columns] = jnp.zeros((pb, 128), bf16)
                    dlo[own, columns] = jnp.zeros((pb, 128), bf16)
                    continue
                picked = jnp.zeros((pb, 128), f32)
                for j in range(nb):
                    tile = y[pl.ds(pl.multiple_of((b * nb + j) * pb, pb), pb), :]
                    picked = jnp.where(side + 2 * m == spots[j], tile, picked)
                hi, lo = halves(picked)
                dhi[own, columns] = hi
                dlo[own, columns] = lo
        return carry

    lax.fori_loop(0, 2, lambda t, carry: band(t * (groups - 1), carry), 0)

    load_cot.wait()
    for g in range(groups):
        cc[:, pl.ds(g * half, half)] = stacked(cot_v[pl.ds(g * half, half), :].T)

    def hop(g, field):
        own = pl.ds(g * half, half)
        near = field[pl.ds(g * half, 3 * half), :]
        both = dot(dhi[own, :], near)
        return both[:, :width] + both[:, width:] + dot(dlo[own, :], near[:, :width])

    def back_hop(k, field):
        total_here = None
        for g in range(max(0, k - 2), min(groups - 1, k) + 1):
            value = field[:, pl.ds(g * half, half)]
            block = (pl.ds(g * half, half), pl.ds((k - g) * half, half))
            both = dot(value, dhi[block])
            term = both[:width] + both[width:] + dot(value[:width], dlo[block])
            total_here = term if total_here is None else total_here + term
        return total_here

    u_out[0] = back_hop(groups + 1, cc)
    u_out[1] = back_hop(0, cc)
    u_swap = swap(1, u_out.at[0], u_out.at[1], u_in)

    lax.fori_loop(1, groups - 1, band, 0)
    load_f.wait()
    fc[pl.ds(half, rows), :] = side_by_side(f_v[...])

    for copy in f_swap:
        copy.wait_recv()
    fc[pl.ds(0, half), :] = side_by_side(f_in[0])
    fc[pl.ds(half + rows, half), :] = side_by_side(f_in[1])
    for slot, g in ((0, groups - 1), (1, 0)):
        first_term = hop(g, fc)
        t_out[slot] = first_term
        tc[pl.ds((g + 1) * half, half), :] = side_by_side(first_term)
    t_swap = swap(2, t_out.at[0], t_out.at[1], t_in)

    for copy in u_swap:
        copy.wait_recv()
    for slot, k in ((0, 1), (1, groups)):
        uc[:, pl.ds((k - 1) * half, half)] = stacked(back_hop(k, cc) + u_in[slot])
    v_out[0] = back_hop(groups + 1, uc)
    v_out[1] = back_hop(0, uc)
    v_swap = swap(3, v_out.at[0], v_out.at[1], v_in)

    for g in range(1, groups - 1):
        tc[pl.ds((g + 1) * half, half), :] = side_by_side(hop(g, fc))
        uc[:, pl.ds(g * half, half)] = stacked(back_hop(g + 1, cc))

    def share(left, right):
        whole = dot(left[...], right[pl.ds(half, rows), :])
        whole = (whole[:width, :width] + whole[width:, width:]) + (
            whole[:width, width:] + whole[width:, :width]
        )
        whole = whole.T
        return whole[:chan] + pltpu.roll(whole[chan:], chan, 1)

    zeroth, one, two = share(cc, fc), share(cc, tc), share(uc, tc)
    left_lanes = lax.broadcasted_iota(jnp.int32, (chan, width), 1) < chan
    top_row = lax.broadcasted_iota(jnp.int32, (chan, width), 0) == 0
    bias_row = jnp.sum(cot_v[...], axis=0, keepdims=True)
    bias_row = bias_row + pltpu.roll(jnp.broadcast_to(bias_row, (8, width)), chan, 1)[:1]
    first_pair = jnp.where(left_lanes, zeroth, pltpu.roll(one, chan, 1))
    second_pair = jnp.where(
        left_lanes, 2.0 * two - zeroth, jnp.where(top_row, bias_row, 0.0)
    )
    rim = 2 * chan // PEERS
    for s in range(PEERS):
        source = first_pair if s < PEERS // 2 else second_pair
        start = (s % (PEERS // 2)) * rim
        grads[s] = source[start : start + rim]
    a_copies = []
    for o, m in enumerate(mates):
        copy = pltpu.make_async_remote_copy(
            src_ref=grads.at[m],
            dst_ref=part_in.at[o],
            send_sem=a_send.at[o],
            recv_sem=a_recv.at[o],
            device_id=at(team * PEERS + m),
            device_id_type=MESH,
        )
        copy.start()
        a_copies.append(copy)

    w0, w1, w2 = w_ref[0], w_ref[1], w_ref[2]
    for k, mixing in enumerate((w0 - w2, w1, 2.0 * w2)):
        hi, lo = halves(both_maps(mixing))
        zero = jnp.zeros_like(lo)
        wf[k] = jnp.concatenate(
            [jnp.concatenate([hi, lo], axis=1), jnp.concatenate([hi, zero], axis=1)], axis=0
        )
        wb[k] = jnp.concatenate(
            [jnp.concatenate([hi, hi], axis=1), jnp.concatenate([lo, zero], axis=1)], axis=0
        )
    bias = jnp.concatenate([b_ref[...], b_ref[...]], axis=1)
    puts = []

    def finish_out(g):
        own = pl.ds((g + 1) * half, half)
        both = dot(fc[own, :], wf[0]) + dot(tc[own, :], wf[1])
        both = both + dot(side_by_side(hop(g, tc)), wf[2])
        here = pl.ds(g * half, half)
        out_v[here, :] = both[:, :width] + both[:, width:] + bias
        copy = pltpu.make_async_copy(out_v.at[here], out_hbm.at[here], put.at[g])
        copy.start()
        puts.append(copy)

    def finish_grad(g, arrived):
        here = pl.ds(g * half, half)
        second = back_hop(g + 1, uc)
        if arrived is not None:
            second = second + arrived
        both = dot(wb[0], cc[:, here]) + dot(wb[1], uc[:, here]) + dot(wb[2], stacked(second))
        ig_v[here, :] = (both[:width] + both[width:]).T
        copy = pltpu.make_async_copy(ig_v.at[here], ig_hbm.at[here], put.at[groups + g])
        copy.start()
        puts.append(copy)

    for g in range(1, groups - 1):
        finish_out(g)
        finish_grad(g, None)

    for copy in a_copies:
        copy.wait_recv()
    summed = grads[rank]
    for o in range(PEERS - 1):
        summed = summed + part_in[o]
    seg[...] = summed
    cross[team] = summed
    b_copies = []
    for o, t in enumerate(others):
        copy = pltpu.make_async_remote_copy(
            src_ref=seg,
            dst_ref=cross.at[team],
            send_sem=b_send.at[o],
            recv_sem=b_recv.at[o],
            device_id=at(t * PEERS + rank),
            device_id_type=MESH,
        )
        copy.start()
        b_copies.append(copy)

    for copy in t_swap:
        copy.wait_recv()
    tc[pl.ds(0, half), :] = side_by_side(t_in[0])
    tc[pl.ds(half + rows, half), :] = side_by_side(t_in[1])
    finish_out(0)
    finish_out(groups - 1)

    for copy in b_copies:
        copy.wait_recv()
    summed = cross[0]
    for t in range(1, teams):
        summed = summed + cross[t]
    summed = summed * scale
    final[rank] = summed
    for copy in b_copies:
        copy.wait_send()
    seg[...] = summed
    c_copies = []
    for o, m in enumerate(mates):
        copy = pltpu.make_async_remote_copy(
            src_ref=seg,
            dst_ref=final.at[rank],
            send_sem=c_send.at[o],
            recv_sem=c_recv.at[o],
            device_id=at(team * PEERS + m),
            device_id_type=MESH,
        )
        copy.start()
        c_copies.append(copy)

    for copy in v_swap:
        copy.wait_recv()
    finish_grad(0, v_in[0])
    finish_grad(groups - 1, v_in[1])

    for copy in c_copies:
        copy.wait_recv()
    for s in range(PEERS):
        piece = final[s]
        start = (s % (PEERS // 2)) * rim
        if s < PEERS // 2:
            wg_ref[0, pl.ds(start, rim), :] = piece[:, :chan]
            wg_ref[1, pl.ds(start, rim), :] = piece[:, chan:]
        else:
            wg_ref[2, pl.ds(start, rim), :] = piece[:, :chan]
    bg_ref[...] = final[PEERS // 2][:1, chan:]

    for copy in f_swap + u_swap + t_swap + v_swap + a_copies + c_copies:
        copy.wait_send()
    for copy in puts:
        copy.wait()


def shards(features, lap_tiles, columns, weights, bias_term, cotangent):
    rows, width = features.shape
    blocks, nb, tile = lap_tiles.shape
    pb = math.isqrt(tile)
    hb = 4
    half = hb * pb
    chan = width // 2
    devices = lax.axis_size("patch") * lax.axis_size("strip")
    teams = devices // PEERS
    rim = 2 * chan // PEERS
    groups = blocks // hb
    scale = 1.0 / math.sqrt(2 * rows * devices)
    vmem = pl.BlockSpec(memory_space=pltpu.VMEM)
    any_space = pl.BlockSpec(memory_space=pl.ANY)
    dma = pltpu.SemaphoreType.DMA
    output, input_grad, weight_grad, bias_grad = pl.pallas_call(
        functools.partial(body, (nb, pb, blocks, hb, blocks * devices, scale)),
        out_shape=(
            jax.ShapeDtypeStruct((rows, width), f32),
            jax.ShapeDtypeStruct((rows, width), f32),
            jax.ShapeDtypeStruct((3, chan, chan), f32),
            jax.ShapeDtypeStruct((1, chan), f32),
        ),
        in_specs=[
            any_space,
            any_space,
            pl.BlockSpec(memory_space=pltpu.SMEM),
            vmem,
            vmem,
            any_space,
        ],
        out_specs=(any_space, any_space, vmem, vmem),
        scratch_shapes=[
            pltpu.VMEM((rows, width), f32),
            pltpu.VMEM((rows, width), f32),
            pltpu.VMEM((nb, blocks, tile), f32),
            pltpu.VMEM((blocks * nb * pb, 128), f32),
            pltpu.VMEM((rows, 3 * half), bf16),
            pltpu.VMEM((rows, 3 * half), bf16),
            pltpu.VMEM((rows + 2 * half, 2 * width), bf16),
            pltpu.VMEM((rows + 2 * half, 2 * width), bf16),
            pltpu.VMEM((2 * width, rows), bf16),
            pltpu.VMEM((2 * width, rows), bf16),
            pltpu.VMEM((3, 2 * width, 2 * width), bf16),
            pltpu.VMEM((3, 2 * width, 2 * width), bf16),
            pltpu.VMEM((rows, width), f32),
            pltpu.VMEM((rows, width), f32),
            pltpu.VMEM((2, half, width), f32),
            pltpu.VMEM((2, half, width), f32),
            pltpu.VMEM((2, width, half), f32),
            pltpu.VMEM((2, width, half), f32),
            pltpu.VMEM((2, half, width), f32),
            pltpu.VMEM((2, width, half), f32),
            pltpu.VMEM((2, width, half), f32),
            pltpu.VMEM((PEERS, rim, width), f32),
            pltpu.VMEM((PEERS - 1, rim, width), f32),
            pltpu.VMEM((rim, width), f32),
            pltpu.VMEM((teams, rim, width), f32),
            pltpu.VMEM((PEERS, rim, width), f32),
            dma((8,)),
            dma((8,)),
            dma((PEERS - 1,)),
            dma((PEERS - 1,)),
            dma((teams - 1,)),
            dma((teams - 1,)),
            dma((PEERS - 1,)),
            dma((PEERS - 1,)),
            dma((3,)),
            dma((2 * groups,)),
        ],
        compiler_params=pltpu.CompilerParams(
            collective_id=0, has_side_effects=True, vmem_limit_bytes=40 * 1024 * 1024
        ),
        name="chebyshev",
    )(
        features,
        jnp.transpose(lap_tiles, (1, 0, 2)),
        columns.T,
        weights,
        bias_term.reshape(1, chan),
        cotangent,
    )
    return output, input_grad, weight_grad, bias_grad.reshape(chan)


def solution(mesh):
    split = ("patch", "strip")
    in_specs = (P(split, None), P(split, None, None), P(split, None), P(), P(), P(split, None))
    out_specs = (P(split, None), P(split, None), P(), P())
    return jax.shard_map(shards, mesh=mesh, in_specs=in_specs, out_specs=out_specs, check_vma=False)
```

```python
import functools
import math

import jax
import jax.numpy as jnp
from jax import lax
from jax.experimental import pallas as pl
from jax.experimental.pallas import tpu as pltpu
from jax.sharding import PartitionSpec as P

MESH = pl.DeviceIdType.MESH
PEERS = 8
f32, bf16 = jnp.float32, jnp.bfloat16


def halves(x):
    hi = x.astype(bf16)
    return hi, (x - hi.astype(f32)).astype(bf16)


def dot(a, b):
    return jnp.dot(a, b, preferred_element_type=f32)


def side_by_side(x):
    return jnp.concatenate(halves(x), axis=1)


def stacked(x):
    return jnp.concatenate(halves(x), axis=0)


def both_maps(w):
    zero = jnp.zeros_like(w)
    return jnp.concatenate(
        [jnp.concatenate([w, zero], axis=1), jnp.concatenate([zero, w], axis=1)], axis=0
    )


def body(
    dims,
    f_hbm, lap_hbm, col_hbm, w_hbm, b_hbm, cot_hbm,
    out_v, ig_v, wg_ref, bg_ref,
    f_v, cot_v, lap_v, col, w_ref, b_ref, y, dhi, dlo, fc, tc, cc, uc, wf, wb,
    f_in, t_in, u_in, v_in, t_out, u_out, v_out,
    grads, part_in, seg, cross, final,
    send, recv, a_send, a_recv, b_send, b_recv, c_send, c_recv, local,
):
    nb, pb, blocks, hb, total, scale = dims
    half, width = hb * pb, f_v.shape[1]
    rows = blocks * pb
    groups = blocks // hb
    chan = width // 2
    strips = lax.axis_size("strip")
    n = lax.axis_size("patch") * strips
    me = lax.axis_index("patch") * strips + lax.axis_index("strip")
    first = me * blocks
    teams = n // PEERS
    team, rank = me // PEERS, me % PEERS

    def at(index):
        return (index // strips, index % strips)

    prev, nxt = at((me + n - 1) % n), at((me + 1) % n)
    mates = [(rank + o) % PEERS for o in range(1, PEERS)]
    others = [(team + o) % teams for o in range(1, teams)]

    barrier = pltpu.get_barrier_semaphore()
    greeted = [prev, nxt]
    greeted += [at(team * PEERS + m) for m in mates]
    greeted += [at(t * PEERS + rank) for t in others]
    for device in greeted:
        pl.semaphore_signal(barrier, inc=1, device_id=device, device_id_type=MESH)
    loads = []
    for src, dst in (
        (lap_hbm, lap_v), (col_hbm, col), (cot_hbm, cot_v), (f_hbm, f_v),
        (w_hbm, w_ref), (b_hbm, b_ref),
    ):
        loads.append(pltpu.make_async_copy(src, dst, local.at[len(loads)]))
        loads[-1].start()
    load_lap, load_col, load_cot, load_f, load_w, load_b = loads

    def swap(slot, to_next, to_prev, landing):
        pair = []
        for i, (src, device) in enumerate(((to_next, nxt), (to_prev, prev))):
            copy = pltpu.make_async_remote_copy(
                src_ref=src,
                dst_ref=landing.at[i],
                send_sem=send.at[2 * slot + i],
                recv_sem=recv.at[2 * slot + i],
                device_id=device,
                device_id_type=MESH,
            )
            copy.start()
            pair.append(copy)
        return pair

    load_lap.wait()
    low = lax.broadcasted_iota(jnp.int32, (8, 128), 1) < pb

    def spread(j, carry):
        for eight in range(blocks // 8):
            for r in range(pb // 2):
                x = lap_v[j, pl.ds(8 * eight, 8), pl.ds(128 * r, 128)]
                turned = pltpu.roll(x, 64, 1)
                start = 8 * eight * apart + j * pb + 2 * r
                y[pl.ds(start, 8, stride=apart), :] = jnp.where(low, x, turned)
                y[pl.ds(start + 1, 8, stride=apart), :] = jnp.where(low, turned, x)
        return carry

    apart = nb * pb + 8
    lax.fori_loop(0, nb, spread, 0)
    pl.semaphore_wait(barrier, len(greeted))
    f_swap = swap(0, f_hbm.at[pl.ds(rows - half, half)], f_hbm.at[pl.ds(0, half)], f_in)

    side = lax.broadcasted_iota(jnp.int32, (8, 128), 1) // pb

    def band(g, carry):
        for i in range(hb):
            b = g * hb + i
            spots = []
            for j in range(nb):
                d = col[j, b] - (first + b - hb)
                d = jnp.where(d < 0, d + total, d)
                d = jnp.where(d >= total, d - total, d)
                spots.append(d + i)
            own = pl.ds(pl.multiple_of(b * pb, pb), pb)
            for m in range(3 * hb // 2):
                columns = pl.ds(128 * m, 128)
                if 2 * m + 1 < i or 2 * m > i + 2 * hb:
                    dhi[own, columns] = jnp.zeros((pb, 128), bf16)
                    dlo[own, columns] = jnp.zeros((pb, 128), bf16)
                    continue
                picked = jnp.zeros((pb // 8, 8, 128), f32)
                for j in range(nb):
                    tile = y[pl.ds(pl.multiple_of(b * apart + j * pb, 8), pb), :]
                    here = jnp.broadcast_to((side == spots[j] - 2 * m)[None], picked.shape)
                    picked = jnp.where(here, tile.reshape(picked.shape), picked)
                hi, lo = halves(picked.reshape(pb, 128))
                dhi[own, columns] = hi
                dlo[own, columns] = lo
        return carry

    load_col.wait()
    lax.fori_loop(0, 2, lambda t, carry: band(t * (groups - 1), carry), 0)

    load_cot.wait()
    for g in range(groups):
        cc[:, pl.ds(g * half, half)] = stacked(cot_v[pl.ds(g * half, half), :].T)

    def hop(g, field):
        own = pl.ds(g * half, half)
        near = field[pl.ds(g * half, 3 * half), :]
        both = dot(dhi[own, :], near)
        return both[:, :width] + both[:, width:] + dot(dlo[own, :], near[:, :width])

    def back_hop(k, field):
        total_here = None
        for g in range(max(0, k - 2), min(groups - 1, k) + 1):
            value = field[:, pl.ds(g * half, half)]
            block = (pl.ds(g * half, half), pl.ds((k - g) * half, half))
            both = dot(value, dhi[block])
            term = both[:width] + both[width:] + dot(value[:width], dlo[block])
            total_here = term if total_here is None else total_here + term
        return total_here

    u_out[0] = back_hop(groups + 1, cc)
    u_out[1] = back_hop(0, cc)
    u_swap = swap(1, u_out.at[0], u_out.at[1], u_in)

    lax.fori_loop(1, groups - 1, band, 0)
    load_w.wait()
    load_b.wait()
    w0, w1, w2 = w_ref[0], w_ref[1], w_ref[2]
    for k, mixing in enumerate((w0 - w2, w1, 2.0 * w2)):
        hi, lo = halves(both_maps(mixing))
        zero = jnp.zeros_like(lo)
        wf[k] = jnp.concatenate(
            [jnp.concatenate([hi, lo], axis=1), jnp.concatenate([hi, zero], axis=1)], axis=0
        )
        wb[k] = jnp.concatenate(
            [jnp.concatenate([hi, hi], axis=1), jnp.concatenate([lo, zero], axis=1)], axis=0
        )
    bias = jnp.concatenate([b_ref[...], b_ref[...]], axis=1)

    load_f.wait()
    fc[pl.ds(half, rows), :] = side_by_side(f_v[...])

    for copy in f_swap:
        copy.wait_recv()
    fc[pl.ds(0, half), :] = side_by_side(f_in[0])
    fc[pl.ds(half + rows, half), :] = side_by_side(f_in[1])
    for slot, g in ((0, groups - 1), (1, 0)):
        first_term = hop(g, fc)
        t_out[slot] = first_term
        tc[pl.ds((g + 1) * half, half), :] = side_by_side(first_term)
    t_swap = swap(2, t_out.at[0], t_out.at[1], t_in)

    for copy in u_swap:
        copy.wait_recv()
    for slot, k in ((0, 1), (1, groups)):
        uc[:, pl.ds((k - 1) * half, half)] = stacked(back_hop(k, cc) + u_in[slot])
    v_out[0] = back_hop(groups + 1, uc)
    v_out[1] = back_hop(0, uc)
    v_swap = swap(3, v_out.at[0], v_out.at[1], v_in)

    for g in range(1, groups - 1):
        tc[pl.ds((g + 1) * half, half), :] = side_by_side(hop(g, fc))
        uc[:, pl.ds(g * half, half)] = stacked(back_hop(g + 1, cc))

    def share(left, right):
        whole = dot(left[...], right[pl.ds(half, rows), :])
        whole = (whole[:width, :width] + whole[width:, width:]) + (
            whole[:width, width:] + whole[width:, :width]
        )
        whole = whole.T
        return whole[:chan] + pltpu.roll(whole[chan:], chan, 1)

    zeroth, one, two = share(cc, fc), share(cc, tc), share(uc, tc)
    left_lanes = lax.broadcasted_iota(jnp.int32, (chan, width), 1) < chan
    top_row = lax.broadcasted_iota(jnp.int32, (chan, width), 0) == 0
    bias_row = jnp.sum(cot_v[...], axis=0, keepdims=True)
    bias_row = bias_row + pltpu.roll(jnp.broadcast_to(bias_row, (8, width)), chan, 1)[:1]
    first_pair = jnp.where(left_lanes, zeroth, pltpu.roll(one, chan, 1))
    second_pair = jnp.where(
        left_lanes, 2.0 * two - zeroth, jnp.where(top_row, bias_row, 0.0)
    )
    rim = 2 * chan // PEERS
    for s in range(PEERS):
        source = first_pair if s < PEERS // 2 else second_pair
        start = (s % (PEERS // 2)) * rim
        grads[s] = source[start : start + rim]
    a_copies = []
    for o, m in enumerate(mates):
        copy = pltpu.make_async_remote_copy(
            src_ref=grads.at[m],
            dst_ref=part_in.at[o],
            send_sem=a_send.at[o],
            recv_sem=a_recv.at[o],
            device_id=at(team * PEERS + m),
            device_id_type=MESH,
        )
        copy.start()
        a_copies.append(copy)

    def finish_out(g):
        own = pl.ds((g + 1) * half, half)
        both = dot(fc[own, :], wf[0]) + dot(tc[own, :], wf[1])
        both = both + dot(side_by_side(hop(g, tc)), wf[2])
        here = pl.ds(g * half, half)
        out_v[here, :] = both[:, :width] + both[:, width:] + bias

    def finish_grad(g, arrived):
        here = pl.ds(g * half, half)
        second = back_hop(g + 1, uc)
        if arrived is not None:
            second = second + arrived
        both = dot(wb[0], cc[:, here]) + dot(wb[1], uc[:, here]) + dot(wb[2], stacked(second))
        ig_v[here, :] = (both[:width] + both[width:]).T

    middle = list(range(1, groups - 1))
    for g in middle[:1]:
        finish_out(g)
        finish_grad(g, None)

    for copy in a_copies:
        copy.wait_recv()
    summed = grads[rank]
    for o in range(PEERS - 1):
        summed = summed + part_in[o]
    seg[...] = summed
    cross[team] = summed
    b_copies = []
    for o, t in enumerate(others):
        copy = pltpu.make_async_remote_copy(
            src_ref=seg,
            dst_ref=cross.at[team],
            send_sem=b_send.at[o],
            recv_sem=b_recv.at[o],
            device_id=at(t * PEERS + rank),
            device_id_type=MESH,
        )
        copy.start()
        b_copies.append(copy)

    for g in middle[1:]:
        finish_out(g)
        finish_grad(g, None)
    for copy in t_swap:
        copy.wait_recv()
    tc[pl.ds(0, half), :] = side_by_side(t_in[0])
    tc[pl.ds(half + rows, half), :] = side_by_side(t_in[1])
    finish_out(0)

    for copy in b_copies:
        copy.wait_recv()
    summed = cross[0]
    for t in range(1, teams):
        summed = summed + cross[t]
    summed = summed * scale
    final[rank] = summed
    for copy in b_copies:
        copy.wait_send()
    seg[...] = summed
    c_copies = []
    for o, m in enumerate(mates):
        copy = pltpu.make_async_remote_copy(
            src_ref=seg,
            dst_ref=final.at[rank],
            send_sem=c_send.at[o],
            recv_sem=c_recv.at[o],
            device_id=at(team * PEERS + m),
            device_id_type=MESH,
        )
        copy.start()
        c_copies.append(copy)

    finish_out(groups - 1)
    for copy in v_swap:
        copy.wait_recv()
    finish_grad(0, v_in[0])
    finish_grad(groups - 1, v_in[1])

    for copy in c_copies:
        copy.wait_recv()
    for s in range(PEERS):
        piece = final[s]
        start = (s % (PEERS // 2)) * rim
        if s < PEERS // 2:
            wg_ref[0, pl.ds(start, rim), :] = piece[:, :chan]
            wg_ref[1, pl.ds(start, rim), :] = piece[:, chan:]
        else:
            wg_ref[2, pl.ds(start, rim), :] = piece[:, :chan]
    bg_ref[...] = final[PEERS // 2][:1, chan:]

    for copy in f_swap + u_swap + t_swap + v_swap + a_copies + c_copies:
        copy.wait_send()


def store(*refs):
    count = len(refs) // 2
    done = refs[-1]
    copies = []
    for i in range(count):
        copies.append(pltpu.make_async_copy(refs[i], refs[count + i], done.at[i]))
        copies[-1].start()
    for copy in copies:
        copy.wait()


def shards(features, lap_tiles, columns, weights, bias_term, cotangent):
    rows, width = features.shape
    blocks, nb, tile = lap_tiles.shape
    pb = math.isqrt(tile)
    hb = 4
    half = hb * pb
    chan = width // 2
    devices = lax.axis_size("patch") * lax.axis_size("strip")
    teams = devices // PEERS
    rim = 2 * chan // PEERS
    scale = 1.0 / math.sqrt(2 * rows * devices)
    vmem = pl.BlockSpec(memory_space=pltpu.VMEM)
    hbm = pl.BlockSpec(memory_space=pltpu.HBM)
    dma = pltpu.SemaphoreType.DMA
    out_shape = (
        jax.ShapeDtypeStruct((rows, width), f32),
        jax.ShapeDtypeStruct((rows, width), f32),
        jax.ShapeDtypeStruct((3, chan, chan), f32),
        jax.ShapeDtypeStruct((1, chan), f32),
    )
    results = pl.pallas_call(
        functools.partial(body, (nb, pb, blocks, hb, blocks * devices, scale)),
        out_shape=tuple(pltpu.VMEM(leaf.shape, leaf.dtype) for leaf in out_shape),
        in_specs=[hbm] * 6,
        out_specs=(vmem,) * 4,
        scratch_shapes=[
            pltpu.VMEM((rows, width), f32),
            pltpu.VMEM((rows, width), f32),
            pltpu.VMEM((nb, blocks, tile), f32),
            pltpu.SMEM((nb, blocks), jnp.int32),
            pltpu.VMEM((3, chan, chan), f32),
            pltpu.VMEM((1, chan), f32),
            pltpu.VMEM((blocks * (nb * pb + 8), 128), f32),
            pltpu.VMEM((rows, 3 * half), bf16),
            pltpu.VMEM((rows, 3 * half), bf16),
            pltpu.VMEM((rows + 2 * half, 2 * width), bf16),
            pltpu.VMEM((rows + 2 * half, 2 * width), bf16),
            pltpu.VMEM((2 * width, rows), bf16),
            pltpu.VMEM((2 * width, rows), bf16),
            pltpu.VMEM((3, 2 * width, 2 * width), bf16),
            pltpu.VMEM((3, 2 * width, 2 * width), bf16),
            pltpu.VMEM((2, half, width), f32),
            pltpu.VMEM((2, half, width), f32),
            pltpu.VMEM((2, width, half), f32),
            pltpu.VMEM((2, width, half), f32),
            pltpu.VMEM((2, half, width), f32),
            pltpu.VMEM((2, width, half), f32),
            pltpu.VMEM((2, width, half), f32),
            pltpu.VMEM((PEERS, rim, width), f32),
            pltpu.VMEM((PEERS - 1, rim, width), f32),
            pltpu.VMEM((rim, width), f32),
            pltpu.VMEM((teams, rim, width), f32),
            pltpu.VMEM((PEERS, rim, width), f32),
            dma((8,)),
            dma((8,)),
            dma((PEERS - 1,)),
            dma((PEERS - 1,)),
            dma((teams - 1,)),
            dma((teams - 1,)),
            dma((PEERS - 1,)),
            dma((PEERS - 1,)),
            dma((6,)),
        ],
        compiler_params=pltpu.CompilerParams(
            collective_id=0, has_side_effects=True, vmem_limit_bytes=60 * 1024 * 1024
        ),
        name="chebyshev",
    )(
        features,
        jnp.transpose(lap_tiles, (1, 0, 2)),
        columns.T,
        weights,
        bias_term.reshape(1, chan),
        cotangent,
    )
    output, input_grad, weight_grad, bias_grad = pl.pallas_call(
        store,
        out_shape=out_shape,
        in_specs=[vmem] * 4,
        out_specs=(hbm,) * 4,
        scratch_shapes=[dma((4,))],
        name="store",
    )(*results)
    return output, input_grad, weight_grad, bias_grad.reshape(chan)


def solution(mesh):
    split = ("patch", "strip")
    in_specs = (P(split, None), P(split, None, None), P(split, None), P(), P(), P(split, None))
    out_specs = (P(split, None), P(split, None), P(), P())
    return jax.shard_map(shards, mesh=mesh, in_specs=in_specs, out_specs=out_specs, check_vma=False)
```

```python
import functools
import math

import jax
import jax.numpy as jnp
from jax import lax
from jax.experimental import pallas as pl
from jax.experimental.pallas import tpu as pltpu
from jax.sharding import PartitionSpec as P

MESH = pl.DeviceIdType.MESH
PEERS = 8
f32, bf16 = jnp.float32, jnp.bfloat16


def halves(x):
    hi = x.astype(bf16)
    return hi, (x - hi.astype(f32)).astype(bf16)


def dot(a, b):
    return jnp.dot(a, b, preferred_element_type=f32)


def side_by_side(x):
    return jnp.concatenate(halves(x), axis=1)


def stacked(x):
    return jnp.concatenate(halves(x), axis=0)


def both_maps(w):
    zero = jnp.zeros_like(w)
    return jnp.concatenate(
        [jnp.concatenate([w, zero], axis=1), jnp.concatenate([zero, w], axis=1)], axis=0
    )


def body(
    dims,
    f_hbm, lap_hbm, col_hbm, w_hbm, b_hbm, cot_hbm,
    out_hbm, ig_hbm, wg_hbm, bg_hbm,
    f_v, cot_v, lap_v, col, w_ref, b_ref, y, dhi, dlo, fc, tc, cc, uc, wf, wb,
    out_v, ig_v, wg_ref, bg_ref,
    f_in, t_in, u_in, v_in, t_out, u_out, v_out,
    grads, part_in, seg, cross, final,
    send, recv, a_send, a_recv, b_send, b_recv, c_send, c_recv, local, tiles, put,
):
    nb, pb, blocks, hb, total, scale = dims
    half, width = hb * pb, f_v.shape[1]
    rows = blocks * pb
    groups = blocks // hb
    chan = width // 2
    strips = lax.axis_size("strip")
    n = lax.axis_size("patch") * strips
    me = lax.axis_index("patch") * strips + lax.axis_index("strip")
    first = me * blocks
    teams = n // PEERS
    team, rank = me // PEERS, me % PEERS

    def at(index):
        return (index // strips, index % strips)

    prev, nxt = at((me + n - 1) % n), at((me + 1) % n)
    mates = [(rank + o) % PEERS for o in range(1, PEERS)]
    others = [(team + o) % teams for o in range(1, teams)]

    barrier = pltpu.get_barrier_semaphore()
    greeted = [prev, nxt]
    greeted += [at(team * PEERS + m) for m in mates]
    greeted += [at(t * PEERS + rank) for t in others]
    for device in greeted:
        pl.semaphore_signal(barrier, inc=1, device_id=device, device_id_type=MESH)
    loads = []
    for src, dst in (
        (cot_hbm, cot_v), (col_hbm, col), (w_hbm, w_ref), (b_hbm, b_ref), (f_hbm, f_v)
    ):
        loads.append(pltpu.make_async_copy(src, dst, local.at[len(loads)]))
    load_cot, load_col, load_w, load_b, load_f = loads
    load_cot.start()
    for j in range(nb):
        pltpu.make_async_copy(lap_hbm.at[j], lap_v.at[j], tiles.at[j]).start()
    for copy in loads[1:]:
        copy.start()

    def swap(slot, to_next, to_prev, landing):
        pair = []
        for i, (src, device) in enumerate(((to_next, nxt), (to_prev, prev))):
            copy = pltpu.make_async_remote_copy(
                src_ref=src,
                dst_ref=landing.at[i],
                send_sem=send.at[2 * slot + i],
                recv_sem=recv.at[2 * slot + i],
                device_id=device,
                device_id_type=MESH,
            )
            copy.start()
            pair.append(copy)
        return pair

    load_cot.wait()
    for g in range(groups):
        cc[:, pl.ds(g * half, half)] = stacked(cot_v[pl.ds(g * half, half), :].T)

    load_w.wait()
    load_b.wait()
    w0, w1, w2 = w_ref[0], w_ref[1], w_ref[2]
    for k, mixing in enumerate((w0 - w2, w1, 2.0 * w2)):
        hi, lo = halves(both_maps(mixing))
        zero = jnp.zeros_like(lo)
        wf[k] = jnp.concatenate(
            [jnp.concatenate([hi, lo], axis=1), jnp.concatenate([hi, zero], axis=1)], axis=0
        )
        wb[k] = jnp.concatenate(
            [jnp.concatenate([hi, hi], axis=1), jnp.concatenate([lo, zero], axis=1)], axis=0
        )
    bias = jnp.concatenate([b_ref[...], b_ref[...]], axis=1)
    load_f.wait()
    fc[pl.ds(half, rows), :] = side_by_side(f_v[...])

    low = lax.broadcasted_iota(jnp.int32, (8, 128), 1) < pb

    def spread(j, carry):
        pltpu.make_async_copy(lap_hbm.at[j], lap_v.at[j], tiles.at[j]).wait()
        for eight in range(blocks // 8):
            for r in range(pb // 2):
                x = lap_v[j, pl.ds(8 * eight, 8), pl.ds(128 * r, 128)]
                turned = pltpu.roll(x, 64, 1)
                start = 8 * eight * apart + j * pb + 2 * r
                y[pl.ds(start, 8, stride=apart), :] = jnp.where(low, x, turned)
                y[pl.ds(start + 1, 8, stride=apart), :] = jnp.where(low, turned, x)
        return carry

    apart = nb * pb + 8
    lax.fori_loop(0, nb, spread, 0)
    pl.semaphore_wait(barrier, len(greeted))
    f_swap = swap(0, f_hbm.at[pl.ds(rows - half, half)], f_hbm.at[pl.ds(0, half)], f_in)

    side = lax.broadcasted_iota(jnp.int32, (8, 128), 1) // pb

    def band(g, carry):
        for i in range(hb):
            b = g * hb + i
            spots = []
            for j in range(nb):
                d = col[j, b] - (first + b - hb)
                d = jnp.where(d < 0, d + total, d)
                d = jnp.where(d >= total, d - total, d)
                spots.append(d + i)
            own = pl.ds(pl.multiple_of(b * pb, pb), pb)
            for m in range(3 * hb // 2):
                columns = pl.ds(128 * m, 128)
                if 2 * m + 1 < i or 2 * m > i + 2 * hb:
                    dhi[own, columns] = jnp.zeros((pb, 128), bf16)
                    dlo[own, columns] = jnp.zeros((pb, 128), bf16)
                    continue
                picked = jnp.zeros((pb // 8, 8, 128), f32)
                for j in range(nb):
                    tile = y[pl.ds(pl.multiple_of(b * apart + j * pb, 8), pb), :]
                    here = jnp.broadcast_to((side == spots[j] - 2 * m)[None], picked.shape)
                    picked = jnp.where(here, tile.reshape(picked.shape), picked)
                hi, lo = halves(picked.reshape(pb, 128))
                dhi[own, columns] = hi
                dlo[own, columns] = lo
        return carry

    load_col.wait()
    lax.fori_loop(0, 2, lambda t, carry: band(t * (groups - 1), carry), 0)

    def hop(g, field):
        own = pl.ds(g * half, half)
        near = field[pl.ds(g * half, 3 * half), :]
        both = dot(dhi[own, :], near)
        return both[:, :width] + both[:, width:] + dot(dlo[own, :], near[:, :width])

    def back_hop(k, field):
        total_here = None
        for g in range(max(0, k - 2), min(groups - 1, k) + 1):
            value = field[:, pl.ds(g * half, half)]
            block = (pl.ds(g * half, half), pl.ds((k - g) * half, half))
            both = dot(value, dhi[block])
            term = both[:width] + both[width:] + dot(value[:width], dlo[block])
            total_here = term if total_here is None else total_here + term
        return total_here

    u_out[0] = back_hop(groups + 1, cc)
    u_out[1] = back_hop(0, cc)
    u_swap = swap(1, u_out.at[0], u_out.at[1], u_in)

    lax.fori_loop(1, groups - 1, band, 0)

    for copy in f_swap:
        copy.wait_recv()
    fc[pl.ds(0, half), :] = side_by_side(f_in[0])
    fc[pl.ds(half + rows, half), :] = side_by_side(f_in[1])
    for slot, g in ((0, groups - 1), (1, 0)):
        first_term = hop(g, fc)
        t_out[slot] = first_term
        tc[pl.ds((g + 1) * half, half), :] = side_by_side(first_term)
    t_swap = swap(2, t_out.at[0], t_out.at[1], t_in)

    for g in range(1, groups - 1):
        tc[pl.ds((g + 1) * half, half), :] = side_by_side(hop(g, fc))
        uc[:, pl.ds(g * half, half)] = stacked(back_hop(g + 1, cc))

    for copy in u_swap:
        copy.wait_recv()
    for slot, k in ((0, 1), (1, groups)):
        uc[:, pl.ds((k - 1) * half, half)] = stacked(back_hop(k, cc) + u_in[slot])
    v_out[0] = back_hop(groups + 1, uc)
    v_out[1] = back_hop(0, uc)
    v_swap = swap(3, v_out.at[0], v_out.at[1], v_in)

    def share(left, right):
        whole = dot(left[...], right[pl.ds(half, rows), :])
        whole = (whole[:width, :width] + whole[width:, width:]) + (
            whole[:width, width:] + whole[width:, :width]
        )
        whole = whole.T
        return whole[:chan] + pltpu.roll(whole[chan:], chan, 1)

    zeroth, one, two = share(cc, fc), share(cc, tc), share(uc, tc)
    left_lanes = lax.broadcasted_iota(jnp.int32, (chan, width), 1) < chan
    top_row = lax.broadcasted_iota(jnp.int32, (chan, width), 0) == 0
    bias_row = jnp.sum(cot_v[...], axis=0, keepdims=True)
    bias_row = bias_row + pltpu.roll(jnp.broadcast_to(bias_row, (8, width)), chan, 1)[:1]
    first_pair = jnp.where(left_lanes, zeroth, pltpu.roll(one, chan, 1))
    second_pair = jnp.where(
        left_lanes, 2.0 * two - zeroth, jnp.where(top_row, bias_row, 0.0)
    )
    rim = 2 * chan // PEERS
    for s in range(PEERS):
        source = first_pair if s < PEERS // 2 else second_pair
        start = (s % (PEERS // 2)) * rim
        grads[s] = source[start : start + rim]
    a_copies = []
    for o, m in enumerate(mates):
        copy = pltpu.make_async_remote_copy(
            src_ref=grads.at[m],
            dst_ref=part_in.at[o],
            send_sem=a_send.at[o],
            recv_sem=a_recv.at[o],
            device_id=at(team * PEERS + m),
            device_id_type=MESH,
        )
        copy.start()
        a_copies.append(copy)

    puts = []

    def write(src, dst):
        copy = pltpu.make_async_copy(src, dst, put.at[len(puts)])
        copy.start()
        puts.append(copy)

    def finish_out(g):
        own = pl.ds((g + 1) * half, half)
        both = dot(fc[own, :], wf[0]) + dot(tc[own, :], wf[1])
        both = both + dot(side_by_side(hop(g, tc)), wf[2])
        here = pl.ds(g * half, half)
        out_v[here, :] = both[:, :width] + both[:, width:] + bias
        write(out_v.at[here], out_hbm.at[here])

    def finish_grad(g, arrived):
        here = pl.ds(g * half, half)
        second = back_hop(g + 1, uc)
        if arrived is not None:
            second = second + arrived
        both = dot(wb[0], cc[:, here]) + dot(wb[1], uc[:, here]) + dot(wb[2], stacked(second))
        ig_v[here, :] = (both[:width] + both[width:]).T
        write(ig_v.at[here], ig_hbm.at[here])

    middle = list(range(1, groups - 1))
    for g in middle:
        finish_out(g)

    for copy in a_copies:
        copy.wait_recv()
    summed = grads[rank]
    for o in range(PEERS - 1):
        summed = summed + part_in[o]
    seg[...] = summed
    cross[team] = summed
    b_copies = []
    for o, t in enumerate(others):
        copy = pltpu.make_async_remote_copy(
            src_ref=seg,
            dst_ref=cross.at[team],
            send_sem=b_send.at[o],
            recv_sem=b_recv.at[o],
            device_id=at(t * PEERS + rank),
            device_id_type=MESH,
        )
        copy.start()
        b_copies.append(copy)

    for g in middle:
        finish_grad(g, None)
    for copy in t_swap:
        copy.wait_recv()
    tc[pl.ds(0, half), :] = side_by_side(t_in[0])
    tc[pl.ds(half + rows, half), :] = side_by_side(t_in[1])
    finish_out(0)

    for copy in b_copies:
        copy.wait_recv()
    summed = cross[0]
    for t in range(1, teams):
        summed = summed + cross[t]
    summed = summed * scale
    final[rank] = summed
    for copy in b_copies:
        copy.wait_send()
    seg[...] = summed
    c_copies = []
    for o, m in enumerate(mates):
        copy = pltpu.make_async_remote_copy(
            src_ref=seg,
            dst_ref=final.at[rank],
            send_sem=c_send.at[o],
            recv_sem=c_recv.at[o],
            device_id=at(team * PEERS + m),
            device_id_type=MESH,
        )
        copy.start()
        c_copies.append(copy)

    finish_out(groups - 1)
    for copy in v_swap:
        copy.wait_recv()
    finish_grad(0, v_in[0])
    finish_grad(groups - 1, v_in[1])

    for copy in c_copies:
        copy.wait_recv()
    for s in range(PEERS):
        piece = final[s]
        start = (s % (PEERS // 2)) * rim
        if s < PEERS // 2:
            wg_ref[0, pl.ds(start, rim), :] = piece[:, :chan]
            wg_ref[1, pl.ds(start, rim), :] = piece[:, chan:]
        else:
            wg_ref[2, pl.ds(start, rim), :] = piece[:, :chan]
    bg_ref[...] = final[PEERS // 2][:1, chan:]
    write(wg_ref, wg_hbm)
    write(bg_ref, bg_hbm)

    for copy in f_swap + u_swap + t_swap + v_swap + a_copies + c_copies:
        copy.wait_send()
    for copy in puts:
        copy.wait()


def store(*refs):
    count = len(refs) // 2
    done = refs[-1]
    copies = []
    for src, dst in zip(refs[:count], refs[count:-1]):
        parts = 4 if src.shape[0] % 32 == 0 else 1
        size = src.shape[0] // parts
        for p in range(parts):
            here = pl.ds(p * size, size)
            copies.append(pltpu.make_async_copy(src.at[here], dst.at[here], done.at[len(copies)]))
            copies[-1].start()
    for copy in copies:
        copy.wait()


def shards(features, lap_tiles, columns, weights, bias_term, cotangent):
    rows, width = features.shape
    blocks, nb, tile = lap_tiles.shape
    pb = math.isqrt(tile)
    hb = 4
    half = hb * pb
    chan = width // 2
    devices = lax.axis_size("patch") * lax.axis_size("strip")
    teams = devices // PEERS
    rim = 2 * chan // PEERS
    scale = 1.0 / math.sqrt(2 * rows * devices)
    hbm = pl.BlockSpec(memory_space=pltpu.HBM)
    dma = pltpu.SemaphoreType.DMA
    out_shape = (
        jax.ShapeDtypeStruct((rows, width), f32),
        jax.ShapeDtypeStruct((rows, width), f32),
        jax.ShapeDtypeStruct((3, chan, chan), f32),
        jax.ShapeDtypeStruct((1, chan), f32),
    )
    results = pl.pallas_call(
        functools.partial(body, (nb, pb, blocks, hb, blocks * devices, scale)),
        out_shape=out_shape,
        in_specs=[hbm] * 6,
        out_specs=(hbm,) * 4,
        scratch_shapes=[
            pltpu.VMEM((rows, width), f32),
            pltpu.VMEM((rows, width), f32),
            pltpu.VMEM((nb, blocks, tile), f32),
            pltpu.SMEM((nb, blocks), jnp.int32),
            pltpu.VMEM((3, chan, chan), f32),
            pltpu.VMEM((1, chan), f32),
            pltpu.VMEM((blocks * (nb * pb + 8), 128), f32),
            pltpu.VMEM((rows, 3 * half), bf16),
            pltpu.VMEM((rows, 3 * half), bf16),
            pltpu.VMEM((rows + 2 * half, 2 * width), bf16),
            pltpu.VMEM((rows + 2 * half, 2 * width), bf16),
            pltpu.VMEM((2 * width, rows), bf16),
            pltpu.VMEM((2 * width, rows), bf16),
            pltpu.VMEM((3, 2 * width, 2 * width), bf16),
            pltpu.VMEM((3, 2 * width, 2 * width), bf16),
            pltpu.VMEM((rows, width), f32),
            pltpu.VMEM((rows, width), f32),
            pltpu.VMEM((3, chan, chan), f32),
            pltpu.VMEM((1, chan), f32),
            pltpu.VMEM((2, half, width), f32),
            pltpu.VMEM((2, half, width), f32),
            pltpu.VMEM((2, width, half), f32),
            pltpu.VMEM((2, width, half), f32),
            pltpu.VMEM((2, half, width), f32),
            pltpu.VMEM((2, width, half), f32),
            pltpu.VMEM((2, width, half), f32),
            pltpu.VMEM((PEERS, rim, width), f32),
            pltpu.VMEM((PEERS - 1, rim, width), f32),
            pltpu.VMEM((rim, width), f32),
            pltpu.VMEM((teams, rim, width), f32),
            pltpu.VMEM((PEERS, rim, width), f32),
            dma((8,)),
            dma((8,)),
            dma((PEERS - 1,)),
            dma((PEERS - 1,)),
            dma((teams - 1,)),
            dma((teams - 1,)),
            dma((PEERS - 1,)),
            dma((PEERS - 1,)),
            dma((5,)),
            dma((nb,)),
            dma((2 * (blocks // hb) + 2,)),
        ],
        compiler_params=pltpu.CompilerParams(
            collective_id=0, has_side_effects=True, vmem_limit_bytes=62 * 1024 * 1024
        ),
        name="chebyshev",
    )(
        features,
        jnp.transpose(lap_tiles, (1, 0, 2)),
        columns.T,
        weights,
        bias_term.reshape(1, chan),
        cotangent,
    )
    output, input_grad, weight_grad, bias_grad = pl.pallas_call(
        store,
        out_shape=out_shape,
        in_specs=[hbm] * 4,
        out_specs=(hbm,) * 4,
        scratch_shapes=[dma((10,))],
        compiler_params=pltpu.CompilerParams(vmem_limit_bytes=62 * 1024 * 1024),
        name="store",
    )(*results)
    return output, input_grad, weight_grad, bias_grad.reshape(chan)


def solution(mesh):
    split = ("patch", "strip")
    in_specs = (P(split, None), P(split, None, None), P(split, None), P(), P(), P(split, None))
    out_specs = (P(split, None), P(split, None), P(), P())
    return jax.shard_map(shards, mesh=mesh, in_specs=in_specs, out_specs=out_specs, check_vma=False)
```

```python
import functools
import math

import jax
import jax.numpy as jnp
from jax import lax
from jax.experimental import pallas as pl
from jax.experimental.pallas import tpu as pltpu
from jax.sharding import PartitionSpec as P

MESH = pl.DeviceIdType.MESH
PEERS = 8
f32, bf16 = jnp.float32, jnp.bfloat16


def halves(x):
    hi = x.astype(bf16)
    return hi, (x - hi.astype(f32)).astype(bf16)


def dot(a, b):
    return jnp.dot(a, b, preferred_element_type=f32)


def side_by_side(x):
    return jnp.concatenate(halves(x), axis=1)


def stacked(x):
    return jnp.concatenate(halves(x), axis=0)


def both_maps(w):
    zero = jnp.zeros_like(w)
    return jnp.concatenate(
        [jnp.concatenate([w, zero], axis=1), jnp.concatenate([zero, w], axis=1)], axis=0
    )


def body(
    dims,
    f_hbm, lap_hbm, col_hbm, w_hbm, b_hbm, cot_hbm,
    out_hbm, ig_hbm, wg_hbm, bg_hbm,
    f_v, cot_v, lap_v, col, w_ref, b_ref, y, dhi, dlo, fc, tc, cc, uc, wf, wb,
    out_v, ig_v, wg_ref, bg_ref,
    f_in, t_in, u_in, v_in, t_out, u_out, v_out,
    grads, part_in, seg, cross, final,
    send, recv, a_send, a_recv, b_send, b_recv, c_send, c_recv, local, tiles, put,
):
    nb, pb, blocks, hb, total, scale = dims
    half, width = hb * pb, f_v.shape[1]
    rows = blocks * pb
    groups = blocks // hb
    chan = width // 2
    strips = lax.axis_size("strip")
    n = lax.axis_size("patch") * strips
    me = lax.axis_index("patch") * strips + lax.axis_index("strip")
    first = me * blocks
    teams = n // PEERS
    team, rank = me // PEERS, me % PEERS

    def at(index):
        return (index // strips, index % strips)

    prev, nxt = at((me + n - 1) % n), at((me + 1) % n)
    mates = [(rank + o) % PEERS for o in range(1, PEERS)]
    others = [(team + o) % teams for o in range(1, teams)]

    barrier = pltpu.get_barrier_semaphore()
    greeted = [prev, nxt]
    greeted += [at(team * PEERS + m) for m in mates]
    greeted += [at(t * PEERS + rank) for t in others]
    for device in greeted:
        pl.semaphore_signal(barrier, inc=1, device_id=device, device_id_type=MESH)
    loads = []
    for src, dst in (
        (cot_hbm, cot_v), (col_hbm, col), (w_hbm, w_ref), (b_hbm, b_ref), (f_hbm, f_v)
    ):
        loads.append(pltpu.make_async_copy(src, dst, local.at[len(loads)]))
    load_cot, load_col, load_w, load_b, load_f = loads
    load_cot.start()
    for j in range(nb):
        pltpu.make_async_copy(lap_hbm.at[j], lap_v.at[j], tiles.at[j]).start()
    for copy in loads[1:]:
        copy.start()

    def swap(slot, to_next, to_prev, landing):
        pair = []
        for i, (src, device) in enumerate(((to_next, nxt), (to_prev, prev))):
            copy = pltpu.make_async_remote_copy(
                src_ref=src,
                dst_ref=landing.at[i],
                send_sem=send.at[2 * slot + i],
                recv_sem=recv.at[2 * slot + i],
                device_id=device,
                device_id_type=MESH,
            )
            copy.start()
            pair.append(copy)
        return pair

    load_cot.wait()
    for g in range(groups):
        cc[:, pl.ds(g * half, half)] = stacked(cot_v[pl.ds(g * half, half), :].T)

    low = lax.broadcasted_iota(jnp.int32, (8, 128), 1) < pb
    apart = nb * pb // 2 + 8

    def spread(pair, carry):
        for j in (2 * pair, 2 * pair + 1):
            pltpu.make_async_copy(lap_hbm.at[j], lap_v.at[j], tiles.at[j]).wait()
        for eight in range(blocks // 8):
            for r in range(pb // 2):
                here = (pl.ds(8 * eight, 8), pl.ds(128 * r, 128))
                a, b = lap_v[(2 * pair, *here)], lap_v[(2 * pair + 1, *here)]
                start = 8 * eight * apart + pair * pb + 2 * r
                even = jnp.where(low, a, pltpu.roll(b, pb, 1))
                odd = jnp.where(low, pltpu.roll(a, pb, 1), b)
                y[pl.ds(start, 8, stride=apart), :] = even
                y[pl.ds(start + 1, 8, stride=apart), :] = odd
        return carry

    lax.fori_loop(0, nb // 2, spread, 0)
    pl.semaphore_wait(barrier, len(greeted))
    f_swap = swap(0, f_hbm.at[pl.ds(rows - half, half)], f_hbm.at[pl.ds(0, half)], f_in)

    side = lax.broadcasted_iota(jnp.int32, (8, 128), 1) // pb

    def band(g, carry):
        for i in range(hb):
            b = g * hb + i
            spots = []
            for j in range(nb):
                d = col[j, b] - (first + b - hb)
                d = jnp.where(d < 0, d + total, d)
                d = jnp.where(d >= total, d - total, d)
                spots.append(d + i)
            ordered, swapped = [], []
            for pair in range(nb // 2):
                near, far = spots[2 * pair], spots[2 * pair + 1]
                ordered.append(jnp.where(low, near, far) - side)
                swapped.append(jnp.where(low, far, near) - side)
            for part in range(pb // 32):
                own = pl.ds(pl.multiple_of(b * pb + 32 * part, 32), 32)
                kept = []
                for pair in range(nb // 2):
                    start = pl.multiple_of(b * apart + pair * pb + 32 * part, 8)
                    tile = y[pl.ds(start, 32), :]
                    kept.append((ordered[pair], tile.reshape(4, 8, 128)))
                    kept.append((swapped[pair], pltpu.roll(tile, pb, 1).reshape(4, 8, 128)))
                for m in range(3 * hb // 2):
                    columns = pl.ds(128 * m, 128)
                    if 2 * m + 1 < i or 2 * m > i + 2 * hb:
                        dhi[own, columns] = jnp.zeros((32, 128), bf16)
                        dlo[own, columns] = jnp.zeros((32, 128), bf16)
                        continue
                    picked = jnp.zeros((4, 8, 128), f32)
                    for spot, tile in kept:
                        here = jnp.broadcast_to((spot == 2 * m)[None], picked.shape)
                        picked = jnp.where(here, tile, picked)
                    hi, lo = halves(picked.reshape(32, 128))
                    dhi[own, columns] = hi
                    dlo[own, columns] = lo
        return carry

    load_col.wait()
    lax.fori_loop(0, 2, lambda t, carry: band(t * (groups - 1), carry), 0)

    def hop(g, field):
        own = pl.ds(g * half, half)
        near = field[pl.ds(g * half, 3 * half), :]
        both = dot(dhi[own, :], near)
        return both[:, :width] + both[:, width:] + dot(dlo[own, :], near[:, :width])

    def back_hop(k, field):
        total_here = None
        for g in range(max(0, k - 2), min(groups - 1, k) + 1):
            value = field[:, pl.ds(g * half, half)]
            block = (pl.ds(g * half, half), pl.ds((k - g) * half, half))
            both = dot(value, dhi[block])
            term = both[:width] + both[width:] + dot(value[:width], dlo[block])
            total_here = term if total_here is None else total_here + term
        return total_here

    u_out[0] = back_hop(groups + 1, cc)
    u_out[1] = back_hop(0, cc)
    u_swap = swap(1, u_out.at[0], u_out.at[1], u_in)

    lax.fori_loop(1, groups - 1, band, 0)
    load_w.wait()
    load_b.wait()
    w0, w1, w2 = w_ref[0], w_ref[1], w_ref[2]
    for k, mixing in enumerate((w0 - w2, w1, 2.0 * w2)):
        hi, lo = halves(both_maps(mixing))
        zero = jnp.zeros_like(lo)
        wf[k] = jnp.concatenate(
            [jnp.concatenate([hi, lo], axis=1), jnp.concatenate([hi, zero], axis=1)], axis=0
        )
        wb[k] = jnp.concatenate(
            [jnp.concatenate([hi, hi], axis=1), jnp.concatenate([lo, zero], axis=1)], axis=0
        )
    bias = jnp.concatenate([b_ref[...], b_ref[...]], axis=1)
    load_f.wait()
    fc[pl.ds(half, rows), :] = side_by_side(f_v[...])

    for copy in f_swap:
        copy.wait_recv()
    fc[pl.ds(0, half), :] = side_by_side(f_in[0])
    fc[pl.ds(half + rows, half), :] = side_by_side(f_in[1])
    for slot, g in ((0, groups - 1), (1, 0)):
        first_term = hop(g, fc)
        t_out[slot] = first_term
        tc[pl.ds((g + 1) * half, half), :] = side_by_side(first_term)
    t_swap = swap(2, t_out.at[0], t_out.at[1], t_in)

    for copy in u_swap:
        copy.wait_recv()
    for slot, k in ((0, 1), (1, groups)):
        uc[:, pl.ds((k - 1) * half, half)] = stacked(back_hop(k, cc) + u_in[slot])
    v_out[0] = back_hop(groups + 1, uc)
    v_out[1] = back_hop(0, uc)
    v_swap = swap(3, v_out.at[0], v_out.at[1], v_in)

    for g in range(1, groups - 1):
        tc[pl.ds((g + 1) * half, half), :] = side_by_side(hop(g, fc))
        uc[:, pl.ds(g * half, half)] = stacked(back_hop(g + 1, cc))

    def share(left, right):
        whole = dot(left[...], right[pl.ds(half, rows), :])
        whole = (whole[:width, :width] + whole[width:, width:]) + (
            whole[:width, width:] + whole[width:, :width]
        )
        whole = whole.T
        return whole[:chan] + pltpu.roll(whole[chan:], chan, 1)

    zeroth, one, two = share(cc, fc), share(cc, tc), share(uc, tc)
    left_lanes = lax.broadcasted_iota(jnp.int32, (chan, width), 1) < chan
    top_row = lax.broadcasted_iota(jnp.int32, (chan, width), 0) == 0
    bias_row = jnp.sum(cot_v[...], axis=0, keepdims=True)
    bias_row = bias_row + pltpu.roll(jnp.broadcast_to(bias_row, (8, width)), chan, 1)[:1]
    first_pair = jnp.where(left_lanes, zeroth, pltpu.roll(one, chan, 1))
    second_pair = jnp.where(
        left_lanes, 2.0 * two - zeroth, jnp.where(top_row, bias_row, 0.0)
    )
    rim = 2 * chan // PEERS
    for s in range(PEERS):
        source = first_pair if s < PEERS // 2 else second_pair
        start = (s % (PEERS // 2)) * rim
        grads[s] = source[start : start + rim]
    a_copies = []
    for o, m in enumerate(mates):
        copy = pltpu.make_async_remote_copy(
            src_ref=grads.at[m],
            dst_ref=part_in.at[o],
            send_sem=a_send.at[o],
            recv_sem=a_recv.at[o],
            device_id=at(team * PEERS + m),
            device_id_type=MESH,
        )
        copy.start()
        a_copies.append(copy)

    puts = []

    def write(src, dst):
        copy = pltpu.make_async_copy(src, dst, put.at[len(puts)])
        copy.start()
        puts.append(copy)

    def finish_out(g):
        own = pl.ds((g + 1) * half, half)
        both = dot(fc[own, :], wf[0]) + dot(tc[own, :], wf[1])
        both = both + dot(side_by_side(hop(g, tc)), wf[2])
        here = pl.ds(g * half, half)
        out_v[here, :] = both[:, :width] + both[:, width:] + bias
        write(out_v.at[here], out_hbm.at[here])

    def finish_grad(g, arrived):
        here = pl.ds(g * half, half)
        second = back_hop(g + 1, uc)
        if arrived is not None:
            second = second + arrived
        both = dot(wb[0], cc[:, here]) + dot(wb[1], uc[:, here]) + dot(wb[2], stacked(second))
        ig_v[here, :] = (both[:width] + both[width:]).T
        write(ig_v.at[here], ig_hbm.at[here])

    middle = list(range(1, groups - 1))
    for g in middle:
        finish_out(g)

    for copy in a_copies:
        copy.wait_recv()
    summed = grads[rank]
    for o in range(PEERS - 1):
        summed = summed + part_in[o]
    seg[...] = summed
    cross[team] = summed
    b_copies = []
    for o, t in enumerate(others):
        copy = pltpu.make_async_remote_copy(
            src_ref=seg,
            dst_ref=cross.at[team],
            send_sem=b_send.at[o],
            recv_sem=b_recv.at[o],
            device_id=at(t * PEERS + rank),
            device_id_type=MESH,
        )
        copy.start()
        b_copies.append(copy)

    for g in middle:
        finish_grad(g, None)
    for copy in t_swap:
        copy.wait_recv()
    tc[pl.ds(0, half), :] = side_by_side(t_in[0])
    tc[pl.ds(half + rows, half), :] = side_by_side(t_in[1])
    finish_out(0)

    for copy in b_copies:
        copy.wait_recv()
    summed = cross[0]
    for t in range(1, teams):
        summed = summed + cross[t]
    summed = summed * scale
    final[rank] = summed
    for copy in b_copies:
        copy.wait_send()
    seg[...] = summed
    c_copies = []
    for o, m in enumerate(mates):
        copy = pltpu.make_async_remote_copy(
            src_ref=seg,
            dst_ref=final.at[rank],
            send_sem=c_send.at[o],
            recv_sem=c_recv.at[o],
            device_id=at(team * PEERS + m),
            device_id_type=MESH,
        )
        copy.start()
        c_copies.append(copy)

    finish_out(groups - 1)
    for copy in v_swap:
        copy.wait_recv()
    finish_grad(0, v_in[0])
    finish_grad(groups - 1, v_in[1])

    for copy in c_copies:
        copy.wait_recv()
    for s in range(PEERS):
        piece = final[s]
        start = (s % (PEERS // 2)) * rim
        if s < PEERS // 2:
            wg_ref[0, pl.ds(start, rim), :] = piece[:, :chan]
            wg_ref[1, pl.ds(start, rim), :] = piece[:, chan:]
        else:
            wg_ref[2, pl.ds(start, rim), :] = piece[:, :chan]
    bg_ref[...] = final[PEERS // 2][:1, chan:]
    write(wg_ref, wg_hbm)
    write(bg_ref, bg_hbm)

    for copy in f_swap + u_swap + t_swap + v_swap + a_copies + c_copies:
        copy.wait_send()
    for copy in puts:
        copy.wait()


def store(*refs):
    count = 4
    sources, targets, held = refs[:count], refs[count : 2 * count], refs[2 * count : 3 * count]
    arrived, done = refs[3 * count :]
    ins, outs = [], []
    for src, dst, mid in zip(sources, targets, held):
        parts = 4 if src.shape[0] % 32 == 0 else 1
        size = src.shape[0] // parts
        for p in range(parts):
            here = pl.ds(p * size, size)
            k = len(ins)
            ins.append(pltpu.make_async_copy(src.at[here], mid.at[here], arrived.at[k]))
            outs.append(pltpu.make_async_copy(mid.at[here], dst.at[here], done.at[k]))
            ins[-1].start()
    for first, second in zip(ins, outs):
        first.wait()
        second.start()
    for copy in outs:
        copy.wait()


def shards(features, lap_tiles, columns, weights, bias_term, cotangent):
    rows, width = features.shape
    blocks, nb, tile = lap_tiles.shape
    pb = math.isqrt(tile)
    hb = 4
    half = hb * pb
    chan = width // 2
    devices = lax.axis_size("patch") * lax.axis_size("strip")
    teams = devices // PEERS
    rim = 2 * chan // PEERS
    scale = 1.0 / math.sqrt(2 * rows * devices)
    hbm = pl.BlockSpec(memory_space=pltpu.HBM)
    dma = pltpu.SemaphoreType.DMA
    out_shape = (
        jax.ShapeDtypeStruct((rows, width), f32),
        jax.ShapeDtypeStruct((rows, width), f32),
        jax.ShapeDtypeStruct((3, chan, chan), f32),
        jax.ShapeDtypeStruct((1, chan), f32),
    )
    results = pl.pallas_call(
        functools.partial(body, (nb, pb, blocks, hb, blocks * devices, scale)),
        out_shape=out_shape,
        in_specs=[hbm] * 6,
        out_specs=(hbm,) * 4,
        scratch_shapes=[
            pltpu.VMEM((rows, width), f32),
            pltpu.VMEM((rows, width), f32),
            pltpu.VMEM((nb, blocks, tile), f32),
            pltpu.SMEM((nb, blocks), jnp.int32),
            pltpu.VMEM((3, chan, chan), f32),
            pltpu.VMEM((1, chan), f32),
            pltpu.VMEM((blocks * (nb * pb // 2 + 8), 128), f32),
            pltpu.VMEM((rows, 3 * half), bf16),
            pltpu.VMEM((rows, 3 * half), bf16),
            pltpu.VMEM((rows + 2 * half, 2 * width), bf16),
            pltpu.VMEM((rows + 2 * half, 2 * width), bf16),
            pltpu.VMEM((2 * width, rows), bf16),
            pltpu.VMEM((2 * width, rows), bf16),
            pltpu.VMEM((3, 2 * width, 2 * width), bf16),
            pltpu.VMEM((3, 2 * width, 2 * width), bf16),
            pltpu.VMEM((rows, width), f32),
            pltpu.VMEM((rows, width), f32),
            pltpu.VMEM((3, chan, chan), f32),
            pltpu.VMEM((1, chan), f32),
            pltpu.VMEM((2, half, width), f32),
            pltpu.VMEM((2, half, width), f32),
            pltpu.VMEM((2, width, half), f32),
            pltpu.VMEM((2, width, half), f32),
            pltpu.VMEM((2, half, width), f32),
            pltpu.VMEM((2, width, half), f32),
            pltpu.VMEM((2, width, half), f32),
            pltpu.VMEM((PEERS, rim, width), f32),
            pltpu.VMEM((PEERS - 1, rim, width), f32),
            pltpu.VMEM((rim, width), f32),
            pltpu.VMEM((teams, rim, width), f32),
            pltpu.VMEM((PEERS, rim, width), f32),
            dma((8,)),
            dma((8,)),
            dma((PEERS - 1,)),
            dma((PEERS - 1,)),
            dma((teams - 1,)),
            dma((teams - 1,)),
            dma((PEERS - 1,)),
            dma((PEERS - 1,)),
            dma((5,)),
            dma((nb,)),
            dma((2 * (blocks // hb) + 2,)),
        ],
        compiler_params=pltpu.CompilerParams(
            collective_id=0, has_side_effects=True, vmem_limit_bytes=62 * 1024 * 1024
        ),
        name="chebyshev",
    )(
        features,
        jnp.transpose(lap_tiles, (1, 0, 2)),
        columns.T,
        weights,
        bias_term.reshape(1, chan),
        cotangent,
    )
    output, input_grad, weight_grad, bias_grad = pl.pallas_call(
        store,
        out_shape=out_shape,
        in_specs=[hbm] * 4,
        out_specs=(hbm,) * 4,
        scratch_shapes=[pltpu.VMEM(leaf.shape, f32) for leaf in out_shape] + [dma((10,))] * 2,
        compiler_params=pltpu.CompilerParams(vmem_limit_bytes=62 * 1024 * 1024),
        name="store",
    )(*results)
    return output, input_grad, weight_grad, bias_grad.reshape(chan)


def solution(mesh):
    split = ("patch", "strip")
    in_specs = (P(split, None), P(split, None, None), P(split, None), P(), P(), P(split, None))
    out_specs = (P(split, None), P(split, None), P(), P())
    return jax.shard_map(shards, mesh=mesh, in_specs=in_specs, out_specs=out_specs, check_vma=False)
```

```python
import functools
import math

import jax
import jax.numpy as jnp
from jax import lax
from jax.experimental import pallas as pl
from jax.experimental.pallas import tpu as pltpu
from jax.sharding import PartitionSpec as P

MESH = pl.DeviceIdType.MESH
PEERS = 8
f32, bf16 = jnp.float32, jnp.bfloat16


def halves(x):
    hi = x.astype(bf16)
    return hi, (x - hi.astype(f32)).astype(bf16)


def dot(a, b):
    return jnp.dot(a, b, preferred_element_type=f32)


def side_by_side(x):
    return jnp.concatenate(halves(x), axis=1)


def stacked(x):
    return jnp.concatenate(halves(x), axis=0)


def both_maps(w):
    zero = jnp.zeros_like(w)
    return jnp.concatenate(
        [jnp.concatenate([w, zero], axis=1), jnp.concatenate([zero, w], axis=1)], axis=0
    )


def body(
    dims,
    f_hbm, lap_hbm, col_hbm, w_hbm, b_hbm, cot_hbm,
    out_hbm, ig_hbm, wg_hbm, bg_hbm,
    f_v, cot_v, lap_v, col, w_ref, b_ref, y, dhi, dlo, fc, tc, cc, uc, wf, wb,
    out_v, ig_v, wg_ref, bg_ref,
    f_in, t_in, u_in, v_in, t_out, u_out, v_out,
    grads, part_in, seg, cross, final,
    send, recv, a_send, a_recv, b_send, b_recv, c_send, c_recv, local, tiles, put,
):
    nb, pb, blocks, hb, total, scale = dims
    half, width = hb * pb, f_v.shape[1]
    rows = blocks * pb
    groups = blocks // hb
    chan = width // 2
    strips = lax.axis_size("strip")
    n = lax.axis_size("patch") * strips
    me = lax.axis_index("patch") * strips + lax.axis_index("strip")
    first = me * blocks
    teams = n // PEERS
    team, rank = me // PEERS, me % PEERS

    def at(index):
        return (index // strips, index % strips)

    prev, nxt = at((me + n - 1) % n), at((me + 1) % n)
    mates = [(rank + o) % PEERS for o in range(1, PEERS)]
    others = [(team + o) % teams for o in range(1, teams)]

    barrier = pltpu.get_barrier_semaphore()
    greeted = [prev, nxt]
    greeted += [at(team * PEERS + m) for m in mates]
    greeted += [at(t * PEERS + rank) for t in others]
    for device in greeted:
        pl.semaphore_signal(barrier, inc=1, device_id=device, device_id_type=MESH)
    loads = []
    for src, dst in (
        (cot_hbm, cot_v), (col_hbm, col), (w_hbm, w_ref), (b_hbm, b_ref), (f_hbm, f_v)
    ):
        loads.append(pltpu.make_async_copy(src, dst, local.at[len(loads)]))
    load_cot, load_col, load_w, load_b, load_f = loads
    load_cot.start()
    for j in range(nb):
        pltpu.make_async_copy(lap_hbm.at[j], lap_v.at[j], tiles.at[j]).start()
    for copy in loads[1:]:
        copy.start()

    def swap(slot, to_next, to_prev, landing):
        pair = []
        for i, (src, device) in enumerate(((to_next, nxt), (to_prev, prev))):
            copy = pltpu.make_async_remote_copy(
                src_ref=src,
                dst_ref=landing.at[i],
                send_sem=send.at[2 * slot + i],
                recv_sem=recv.at[2 * slot + i],
                device_id=device,
                device_id_type=MESH,
            )
            copy.start()
            pair.append(copy)
        return pair

    load_cot.wait()
    for g in range(groups):
        cc[:, pl.ds(g * half, half)] = stacked(cot_v[pl.ds(g * half, half), :].T)

    pl.semaphore_wait(barrier, len(greeted))
    f_swap = swap(0, f_hbm.at[pl.ds(rows - half, half)], f_hbm.at[pl.ds(0, half)], f_in)

    low = lax.broadcasted_iota(jnp.int32, (8, 128), 1) < pb
    apart = nb * pb // 2 + 8

    def spread(pair, carry):
        for j in (2 * pair, 2 * pair + 1):
            pltpu.make_async_copy(lap_hbm.at[j], lap_v.at[j], tiles.at[j]).wait()
        for eight in range(blocks // 8):
            for r in range(pb // 2):
                here = (pl.ds(8 * eight, 8), pl.ds(128 * r, 128))
                a, b = lap_v[(2 * pair, *here)], lap_v[(2 * pair + 1, *here)]
                start = 8 * eight * apart + pair * pb + 2 * r
                even = jnp.where(low, a, pltpu.roll(b, pb, 1))
                odd = jnp.where(low, pltpu.roll(a, pb, 1), b)
                y[pl.ds(start, 8, stride=apart), :] = even
                y[pl.ds(start + 1, 8, stride=apart), :] = odd
        return carry

    lax.fori_loop(0, nb // 2, spread, 0)

    side = lax.broadcasted_iota(jnp.int32, (8, 128), 1) // pb

    def band(g, carry):
        for i in range(hb):
            b = g * hb + i
            spots = []
            for j in range(nb):
                d = col[j, b] - (first + b - hb)
                d = jnp.where(d < 0, d + total, d)
                d = jnp.where(d >= total, d - total, d)
                spots.append(d + i)
            ordered, swapped = [], []
            for pair in range(nb // 2):
                near, far = spots[2 * pair], spots[2 * pair + 1]
                ordered.append(jnp.where(low, near, far) - side)
                swapped.append(jnp.where(low, far, near) - side)
            for part in range(pb // 32):
                own = pl.ds(pl.multiple_of(b * pb + 32 * part, 32), 32)
                kept = []
                for pair in range(nb // 2):
                    start = pl.multiple_of(b * apart + pair * pb + 32 * part, 8)
                    tile = y[pl.ds(start, 32), :]
                    kept.append((ordered[pair], tile.reshape(4, 8, 128)))
                    kept.append((swapped[pair], pltpu.roll(tile, pb, 1).reshape(4, 8, 128)))
                for m in range(3 * hb // 2):
                    columns = pl.ds(128 * m, 128)
                    if 2 * m + 1 < i or 2 * m > i + 2 * hb:
                        dhi[own, columns] = jnp.zeros((32, 128), bf16)
                        dlo[own, columns] = jnp.zeros((32, 128), bf16)
                        continue
                    picked = jnp.zeros((4, 8, 128), f32)
                    for spot, tile in kept:
                        here = jnp.broadcast_to((spot == 2 * m)[None], picked.shape)
                        picked = jnp.where(here, tile, picked)
                    hi, lo = halves(picked.reshape(32, 128))
                    dhi[own, columns] = hi
                    dlo[own, columns] = lo
        return carry

    load_col.wait()
    lax.fori_loop(0, 2, lambda t, carry: band(t * (groups - 1), carry), 0)

    def hop(g, field):
        own = pl.ds(g * half, half)
        near = field[pl.ds(g * half, 3 * half), :]
        both = dot(dhi[own, :], near)
        return both[:, :width] + both[:, width:] + dot(dlo[own, :], near[:, :width])

    def back_hop(k, field):
        total_here = None
        for g in range(max(0, k - 2), min(groups - 1, k) + 1):
            value = field[:, pl.ds(g * half, half)]
            block = (pl.ds(g * half, half), pl.ds((k - g) * half, half))
            both = dot(value, dhi[block])
            term = both[:width] + both[width:] + dot(value[:width], dlo[block])
            total_here = term if total_here is None else total_here + term
        return total_here

    u_out[0] = back_hop(groups + 1, cc)
    u_out[1] = back_hop(0, cc)
    u_swap = swap(1, u_out.at[0], u_out.at[1], u_in)

    load_f.wait()
    fc[pl.ds(half, rows), :] = side_by_side(f_v[...])

    for copy in f_swap:
        copy.wait_recv()
    fc[pl.ds(0, half), :] = side_by_side(f_in[0])
    fc[pl.ds(half + rows, half), :] = side_by_side(f_in[1])
    for slot, g in ((0, groups - 1), (1, 0)):
        first_term = hop(g, fc)
        t_out[slot] = first_term
        tc[pl.ds((g + 1) * half, half), :] = side_by_side(first_term)
    t_swap = swap(2, t_out.at[0], t_out.at[1], t_in)
    lax.fori_loop(1, groups - 1, band, 0)
    load_w.wait()
    load_b.wait()
    w0, w1, w2 = w_ref[0], w_ref[1], w_ref[2]
    for k, mixing in enumerate((w0 - w2, w1, 2.0 * w2)):
        hi, lo = halves(both_maps(mixing))
        zero = jnp.zeros_like(lo)
        wf[k] = jnp.concatenate(
            [jnp.concatenate([hi, lo], axis=1), jnp.concatenate([hi, zero], axis=1)], axis=0
        )
        wb[k] = jnp.concatenate(
            [jnp.concatenate([hi, hi], axis=1), jnp.concatenate([lo, zero], axis=1)], axis=0
        )
    bias = jnp.concatenate([b_ref[...], b_ref[...]], axis=1)

    for copy in u_swap:
        copy.wait_recv()
    for slot, k in ((0, 1), (1, groups)):
        uc[:, pl.ds((k - 1) * half, half)] = stacked(back_hop(k, cc) + u_in[slot])
    v_out[0] = back_hop(groups + 1, uc)
    v_out[1] = back_hop(0, uc)
    v_swap = swap(3, v_out.at[0], v_out.at[1], v_in)

    for g in range(1, groups - 1):
        tc[pl.ds((g + 1) * half, half), :] = side_by_side(hop(g, fc))
        uc[:, pl.ds(g * half, half)] = stacked(back_hop(g + 1, cc))

    def share(left, right):
        whole = dot(left[...], right[pl.ds(half, rows), :])
        whole = (whole[:width, :width] + whole[width:, width:]) + (
            whole[:width, width:] + whole[width:, :width]
        )
        whole = whole.T
        return whole[:chan] + pltpu.roll(whole[chan:], chan, 1)

    zeroth, one, two = share(cc, fc), share(cc, tc), share(uc, tc)
    left_lanes = lax.broadcasted_iota(jnp.int32, (chan, width), 1) < chan
    top_row = lax.broadcasted_iota(jnp.int32, (chan, width), 0) == 0
    bias_row = jnp.sum(cot_v[...], axis=0, keepdims=True)
    bias_row = bias_row + pltpu.roll(jnp.broadcast_to(bias_row, (8, width)), chan, 1)[:1]
    first_pair = jnp.where(left_lanes, zeroth, pltpu.roll(one, chan, 1))
    second_pair = jnp.where(
        left_lanes, 2.0 * two - zeroth, jnp.where(top_row, bias_row, 0.0)
    )
    rim = 2 * chan // PEERS
    for s in range(PEERS):
        source = first_pair if s < PEERS // 2 else second_pair
        start = (s % (PEERS // 2)) * rim
        grads[s] = source[start : start + rim]
    a_copies = []
    for o, m in enumerate(mates):
        copy = pltpu.make_async_remote_copy(
            src_ref=grads.at[m],
            dst_ref=part_in.at[o],
            send_sem=a_send.at[o],
            recv_sem=a_recv.at[o],
            device_id=at(team * PEERS + m),
            device_id_type=MESH,
        )
        copy.start()
        a_copies.append(copy)

    puts = []

    def write(src, dst):
        copy = pltpu.make_async_copy(src, dst, put.at[len(puts)])
        copy.start()
        puts.append(copy)

    def finish_out(g):
        own = pl.ds((g + 1) * half, half)
        both = dot(fc[own, :], wf[0]) + dot(tc[own, :], wf[1])
        both = both + dot(side_by_side(hop(g, tc)), wf[2])
        here = pl.ds(g * half, half)
        out_v[here, :] = both[:, :width] + both[:, width:] + bias
        write(out_v.at[here], out_hbm.at[here])

    def finish_grad(g, arrived):
        here = pl.ds(g * half, half)
        second = back_hop(g + 1, uc)
        if arrived is not None:
            second = second + arrived
        both = dot(wb[0], cc[:, here]) + dot(wb[1], uc[:, here]) + dot(wb[2], stacked(second))
        ig_v[here, :] = (both[:width] + both[width:]).T
        write(ig_v.at[here], ig_hbm.at[here])

    middle = list(range(1, groups - 1))
    for g in middle:
        finish_out(g)

    for copy in a_copies:
        copy.wait_recv()
    summed = grads[rank]
    for o in range(PEERS - 1):
        summed = summed + part_in[o]
    seg[...] = summed
    cross[team] = summed
    b_copies = []
    for o, t in enumerate(others):
        copy = pltpu.make_async_remote_copy(
            src_ref=seg,
            dst_ref=cross.at[team],
            send_sem=b_send.at[o],
            recv_sem=b_recv.at[o],
            device_id=at(t * PEERS + rank),
            device_id_type=MESH,
        )
        copy.start()
        b_copies.append(copy)

    for g in middle:
        finish_grad(g, None)
    for copy in t_swap:
        copy.wait_recv()
    tc[pl.ds(0, half), :] = side_by_side(t_in[0])
    tc[pl.ds(half + rows, half), :] = side_by_side(t_in[1])
    finish_out(0)

    for copy in b_copies:
        copy.wait_recv()
    summed = cross[0]
    for t in range(1, teams):
        summed = summed + cross[t]
    summed = summed * scale
    final[rank] = summed
    for copy in b_copies:
        copy.wait_send()
    seg[...] = summed
    c_copies = []
    for o, m in enumerate(mates):
        copy = pltpu.make_async_remote_copy(
            src_ref=seg,
            dst_ref=final.at[rank],
            send_sem=c_send.at[o],
            recv_sem=c_recv.at[o],
            device_id=at(team * PEERS + m),
            device_id_type=MESH,
        )
        copy.start()
        c_copies.append(copy)

    finish_out(groups - 1)
    for copy in v_swap:
        copy.wait_recv()
    finish_grad(0, v_in[0])
    finish_grad(groups - 1, v_in[1])

    for copy in c_copies:
        copy.wait_recv()
    for s in range(PEERS):
        piece = final[s]
        start = (s % (PEERS // 2)) * rim
        if s < PEERS // 2:
            wg_ref[0, pl.ds(start, rim), :] = piece[:, :chan]
            wg_ref[1, pl.ds(start, rim), :] = piece[:, chan:]
        else:
            wg_ref[2, pl.ds(start, rim), :] = piece[:, :chan]
    bg_ref[...] = final[PEERS // 2][:1, chan:]
    write(wg_ref, wg_hbm)
    write(bg_ref, bg_hbm)

    for copy in f_swap + u_swap + t_swap + v_swap + a_copies + c_copies:
        copy.wait_send()
    for copy in puts:
        copy.wait()


def store(*refs):
    count = 4
    sources, targets, held = refs[:count], refs[count : 2 * count], refs[2 * count : 3 * count]
    arrived, done = refs[3 * count :]
    ins, outs = [], []
    for src, dst, mid in zip(sources, targets, held):
        parts = 4 if src.shape[0] % 32 == 0 else 1
        size = src.shape[0] // parts
        for p in range(parts):
            here = pl.ds(p * size, size)
            k = len(ins)
            ins.append(pltpu.make_async_copy(src.at[here], mid.at[here], arrived.at[k]))
            outs.append(pltpu.make_async_copy(mid.at[here], dst.at[here], done.at[k]))
            ins[-1].start()
    for first, second in zip(ins, outs):
        first.wait()
        second.start()
    for copy in outs:
        copy.wait()


def shards(features, lap_tiles, columns, weights, bias_term, cotangent):
    rows, width = features.shape
    blocks, nb, tile = lap_tiles.shape
    pb = math.isqrt(tile)
    hb = 4
    half = hb * pb
    chan = width // 2
    devices = lax.axis_size("patch") * lax.axis_size("strip")
    teams = devices // PEERS
    rim = 2 * chan // PEERS
    scale = 1.0 / math.sqrt(2 * rows * devices)
    hbm = pl.BlockSpec(memory_space=pltpu.HBM)
    dma = pltpu.SemaphoreType.DMA
    out_shape = (
        jax.ShapeDtypeStruct((rows, width), f32),
        jax.ShapeDtypeStruct((rows, width), f32),
        jax.ShapeDtypeStruct((3, chan, chan), f32),
        jax.ShapeDtypeStruct((1, chan), f32),
    )
    results = pl.pallas_call(
        functools.partial(body, (nb, pb, blocks, hb, blocks * devices, scale)),
        out_shape=out_shape,
        in_specs=[hbm] * 6,
        out_specs=(hbm,) * 4,
        scratch_shapes=[
            pltpu.VMEM((rows, width), f32),
            pltpu.VMEM((rows, width), f32),
            pltpu.VMEM((nb, blocks, tile), f32),
            pltpu.SMEM((nb, blocks), jnp.int32),
            pltpu.VMEM((3, chan, chan), f32),
            pltpu.VMEM((1, chan), f32),
            pltpu.VMEM((blocks * (nb * pb // 2 + 8), 128), f32),
            pltpu.VMEM((rows, 3 * half), bf16),
            pltpu.VMEM((rows, 3 * half), bf16),
            pltpu.VMEM((rows + 2 * half, 2 * width), bf16),
            pltpu.VMEM((rows + 2 * half, 2 * width), bf16),
            pltpu.VMEM((2 * width, rows), bf16),
            pltpu.VMEM((2 * width, rows), bf16),
            pltpu.VMEM((3, 2 * width, 2 * width), bf16),
            pltpu.VMEM((3, 2 * width, 2 * width), bf16),
            pltpu.VMEM((rows, width), f32),
            pltpu.VMEM((rows, width), f32),
            pltpu.VMEM((3, chan, chan), f32),
            pltpu.VMEM((1, chan), f32),
            pltpu.VMEM((2, half, width), f32),
            pltpu.VMEM((2, half, width), f32),
            pltpu.VMEM((2, width, half), f32),
            pltpu.VMEM((2, width, half), f32),
            pltpu.VMEM((2, half, width), f32),
            pltpu.VMEM((2, width, half), f32),
            pltpu.VMEM((2, width, half), f32),
            pltpu.VMEM((PEERS, rim, width), f32),
            pltpu.VMEM((PEERS - 1, rim, width), f32),
            pltpu.VMEM((rim, width), f32),
            pltpu.VMEM((teams, rim, width), f32),
            pltpu.VMEM((PEERS, rim, width), f32),
            dma((8,)),
            dma((8,)),
            dma((PEERS - 1,)),
            dma((PEERS - 1,)),
            dma((teams - 1,)),
            dma((teams - 1,)),
            dma((PEERS - 1,)),
            dma((PEERS - 1,)),
            dma((5,)),
            dma((nb,)),
            dma((2 * (blocks // hb) + 2,)),
        ],
        compiler_params=pltpu.CompilerParams(
            collective_id=0, has_side_effects=True, vmem_limit_bytes=62 * 1024 * 1024
        ),
        name="chebyshev",
    )(
        features,
        jnp.transpose(lap_tiles, (1, 0, 2)),
        columns.T,
        weights,
        bias_term.reshape(1, chan),
        cotangent,
    )
    output, input_grad, weight_grad, bias_grad = pl.pallas_call(
        store,
        out_shape=out_shape,
        in_specs=[hbm] * 4,
        out_specs=(hbm,) * 4,
        scratch_shapes=[pltpu.VMEM(leaf.shape, f32) for leaf in out_shape] + [dma((10,))] * 2,
        compiler_params=pltpu.CompilerParams(vmem_limit_bytes=62 * 1024 * 1024),
        name="store",
    )(*results)
    return output, input_grad, weight_grad, bias_grad.reshape(chan)


def solution(mesh):
    split = ("patch", "strip")
    in_specs = (P(split, None), P(split, None, None), P(split, None), P(), P(), P(split, None))
    out_specs = (P(split, None), P(split, None), P(), P())
    return jax.shard_map(shards, mesh=mesh, in_specs=in_specs, out_specs=out_specs, check_vma=False)
```

```python
import functools
import math

import jax
import jax.numpy as jnp
from jax import lax
from jax.experimental import pallas as pl
from jax.experimental.pallas import tpu as pltpu
from jax.sharding import PartitionSpec as P

MESH = pl.DeviceIdType.MESH
PEERS = 8
f32, bf16 = jnp.float32, jnp.bfloat16


def halves(x):
    hi = x.astype(bf16)
    return hi, (x - hi.astype(f32)).astype(bf16)


def dot(a, b):
    return jnp.dot(a, b, preferred_element_type=f32)


def side_by_side(x):
    return jnp.concatenate(halves(x), axis=1)


def stacked(x):
    return jnp.concatenate(halves(x), axis=0)


def both_maps(w):
    zero = jnp.zeros_like(w)
    return jnp.concatenate(
        [jnp.concatenate([w, zero], axis=1), jnp.concatenate([zero, w], axis=1)], axis=0
    )


def body(
    dims,
    f_hbm, lap_hbm, col_hbm, w_hbm, b_hbm, cot_hbm,
    out_hbm, ig_hbm, wg_hbm, bg_hbm,
    f_v, cot_v, lap_v, col, w_ref, b_ref, y, dd, fc, tc, cc, uc, wf, wb,
    out_v, ig_v, wg_ref, bg_ref,
    f_in, t_in, u_in, v_in, t_out, u_out, v_out,
    grads, part_in, seg, cross, final,
    send, recv, a_send, a_recv, b_send, b_recv, c_send, c_recv, local, tiles, put,
):
    nb, pb, blocks, hb, total, scale = dims
    half, width = hb * pb, f_v.shape[1]
    rows = blocks * pb
    groups = blocks // hb
    chan = width // 2
    strips = lax.axis_size("strip")
    n = lax.axis_size("patch") * strips
    me = lax.axis_index("patch") * strips + lax.axis_index("strip")
    first = me * blocks
    teams = n // PEERS
    team, rank = me // PEERS, me % PEERS

    def at(index):
        return (index // strips, index % strips)

    prev, nxt = at((me + n - 1) % n), at((me + 1) % n)
    mates = [(rank + o) % PEERS for o in range(1, PEERS)]
    others = [(team + o) % teams for o in range(1, teams)]

    barrier = pltpu.get_barrier_semaphore()
    greeted = [prev, nxt]
    greeted += [at(team * PEERS + m) for m in mates]
    greeted += [at(t * PEERS + rank) for t in others]
    for device in greeted:
        pl.semaphore_signal(barrier, inc=1, device_id=device, device_id_type=MESH)
    loads = []
    for src, dst in (
        (cot_hbm, cot_v), (col_hbm, col), (w_hbm, w_ref), (b_hbm, b_ref), (f_hbm, f_v)
    ):
        loads.append(pltpu.make_async_copy(src, dst, local.at[len(loads)]))
    load_cot, load_col, load_w, load_b, load_f = loads
    load_cot.start()
    for j in range(nb):
        pltpu.make_async_copy(lap_hbm.at[j], lap_v.at[j], tiles.at[j]).start()
    for copy in loads[1:]:
        copy.start()

    def swap(slot, to_next, to_prev, landing):
        pair = []
        for i, (src, device) in enumerate(((to_next, nxt), (to_prev, prev))):
            copy = pltpu.make_async_remote_copy(
                src_ref=src,
                dst_ref=landing.at[i],
                send_sem=send.at[2 * slot + i],
                recv_sem=recv.at[2 * slot + i],
                device_id=device,
                device_id_type=MESH,
            )
            copy.start()
            pair.append(copy)
        return pair

    load_cot.wait()
    for g in range(groups):
        cc[:, pl.ds(g * half, half)] = stacked(cot_v[pl.ds(g * half, half), :].T)

    pl.semaphore_wait(barrier, len(greeted))
    f_swap = swap(0, f_hbm.at[pl.ds(rows - half, half)], f_hbm.at[pl.ds(0, half)], f_in)

    low = lax.broadcasted_iota(jnp.int32, (8, 128), 1) < pb
    apart = nb * pb // 2 + 8

    def spread(pair, carry):
        for j in (2 * pair, 2 * pair + 1):
            pltpu.make_async_copy(lap_hbm.at[j], lap_v.at[j], tiles.at[j]).wait()
        for eight in range(blocks // 8):
            for r in range(pb // 2):
                here = (pl.ds(8 * eight, 8), pl.ds(128 * r, 128))
                a, b = lap_v[(2 * pair, *here)], lap_v[(2 * pair + 1, *here)]
                start = 8 * eight * apart + pair * pb + 2 * r
                even = jnp.where(low, a, pltpu.roll(b, pb, 1))
                odd = jnp.where(low, pltpu.roll(a, pb, 1), b)
                y[pl.ds(start, 8, stride=apart), :] = even
                y[pl.ds(start + 1, 8, stride=apart), :] = odd
        return carry

    lax.fori_loop(0, nb // 2, spread, 0)

    side = lax.broadcasted_iota(jnp.int32, (8, 128), 1) // pb

    def band(g, carry):
        for i in range(hb):
            b = g * hb + i
            spots = []
            for j in range(nb):
                d = col[j, b] - (first + b - hb)
                d = jnp.where(d < 0, d + total, d)
                d = jnp.where(d >= total, d - total, d)
                spots.append(d + i)
            ordered, swapped = [], []
            for pair in range(nb // 2):
                near, far = spots[2 * pair], spots[2 * pair + 1]
                ordered.append(jnp.where(low, near, far) - side)
                swapped.append(jnp.where(low, far, near) - side)
            for part in range(pb // 32):
                top = g * 2 * half + i * pb + 32 * part
                own = pl.ds(pl.multiple_of(top, 32), 32)
                own_low = pl.ds(pl.multiple_of(top + half, 32), 32)
                kept = []
                for pair in range(nb // 2):
                    start = pl.multiple_of(b * apart + pair * pb + 32 * part, 8)
                    tile = y[pl.ds(start, 32), :]
                    kept.append((ordered[pair], tile.reshape(4, 8, 128)))
                    kept.append((swapped[pair], pltpu.roll(tile, pb, 1).reshape(4, 8, 128)))
                for m in range(3 * hb // 2):
                    columns = pl.ds(128 * m, 128)
                    if 2 * m + 1 < i or 2 * m > i + 2 * hb:
                        dd[own, columns] = jnp.zeros((32, 128), bf16)
                        dd[own_low, columns] = jnp.zeros((32, 128), bf16)
                        continue
                    picked = jnp.zeros((4, 8, 128), f32)
                    for spot, tile in kept:
                        here = jnp.broadcast_to((spot == 2 * m)[None], picked.shape)
                        picked = jnp.where(here, tile, picked)
                    hi, lo = halves(picked.reshape(32, 128))
                    dd[own, columns] = hi
                    dd[own_low, columns] = lo
        return carry

    load_col.wait()
    lax.fori_loop(0, 2, lambda t, carry: band(t * (groups - 1), carry), 0)

    def hop(g, field):
        both = dot(dd[pl.ds(g * 2 * half, 2 * half), :], field[pl.ds(g * half, 3 * half), :])
        return both[:half, :width] + (both[:half, width:] + both[half:, :width])

    def back_hop(k, field):
        total_here = None
        for g in range(max(0, k - 2), min(groups - 1, k) + 1):
            value = field[:, pl.ds(g * half, half)]
            block = pl.ds((k - g) * half, half)
            both = dot(value, dd[pl.ds(2 * g * half, half), block])
            low_part = dot(value[:width], dd[pl.ds((2 * g + 1) * half, half), block])
            term = both[:width] + both[width:] + low_part
            total_here = term if total_here is None else total_here + term
        return total_here

    u_out[0] = back_hop(groups + 1, cc)
    u_out[1] = back_hop(0, cc)
    u_swap = swap(1, u_out.at[0], u_out.at[1], u_in)

    load_f.wait()
    fc[pl.ds(half, rows), :] = side_by_side(f_v[...])

    for copy in f_swap:
        copy.wait_recv()
    fc[pl.ds(0, half), :] = side_by_side(f_in[0])
    fc[pl.ds(half + rows, half), :] = side_by_side(f_in[1])
    for slot, g in ((0, groups - 1), (1, 0)):
        first_term = hop(g, fc)
        t_out[slot] = first_term
        tc[pl.ds((g + 1) * half, half), :] = side_by_side(first_term)
    t_swap = swap(2, t_out.at[0], t_out.at[1], t_in)
    lax.fori_loop(1, groups - 1, band, 0)
    load_w.wait()
    load_b.wait()
    w0, w1, w2 = w_ref[0], w_ref[1], w_ref[2]
    for k, mixing in enumerate((w0 - w2, w1, 2.0 * w2)):
        hi, lo = halves(both_maps(mixing))
        zero = jnp.zeros_like(lo)
        wf[k] = jnp.concatenate(
            [jnp.concatenate([hi, lo], axis=1), jnp.concatenate([hi, zero], axis=1)], axis=0
        )
        wb[k] = jnp.concatenate(
            [jnp.concatenate([hi, hi], axis=1), jnp.concatenate([lo, zero], axis=1)], axis=0
        )
    bias = jnp.concatenate([b_ref[...], b_ref[...]], axis=1)

    for copy in u_swap:
        copy.wait_recv()
    for slot, k in ((0, 1), (1, groups)):
        uc[:, pl.ds((k - 1) * half, half)] = stacked(back_hop(k, cc) + u_in[slot])
    v_out[0] = back_hop(groups + 1, uc)
    v_out[1] = back_hop(0, uc)
    v_swap = swap(3, v_out.at[0], v_out.at[1], v_in)

    for g in range(1, groups - 1):
        tc[pl.ds((g + 1) * half, half), :] = side_by_side(hop(g, fc))
        uc[:, pl.ds(g * half, half)] = stacked(back_hop(g + 1, cc))

    def share(left, right):
        whole = dot(left[...], right[pl.ds(half, rows), :])
        whole = (whole[:width, :width] + whole[width:, width:]) + (
            whole[:width, width:] + whole[width:, :width]
        )
        whole = whole.T
        return whole[:chan] + pltpu.roll(whole[chan:], chan, 1)

    zeroth, one, two = share(cc, fc), share(cc, tc), share(uc, tc)
    left_lanes = lax.broadcasted_iota(jnp.int32, (chan, width), 1) < chan
    top_row = lax.broadcasted_iota(jnp.int32, (chan, width), 0) == 0
    bias_row = jnp.sum(cot_v[...], axis=0, keepdims=True)
    bias_row = bias_row + pltpu.roll(jnp.broadcast_to(bias_row, (8, width)), chan, 1)[:1]
    first_pair = jnp.where(left_lanes, zeroth, pltpu.roll(one, chan, 1))
    second_pair = jnp.where(
        left_lanes, 2.0 * two - zeroth, jnp.where(top_row, bias_row, 0.0)
    )
    rim = 2 * chan // PEERS
    for s in range(PEERS):
        source = first_pair if s < PEERS // 2 else second_pair
        start = (s % (PEERS // 2)) * rim
        grads[s] = source[start : start + rim]
    a_copies = []
    for o, m in enumerate(mates):
        copy = pltpu.make_async_remote_copy(
            src_ref=grads.at[m],
            dst_ref=part_in.at[o],
            send_sem=a_send.at[o],
            recv_sem=a_recv.at[o],
            device_id=at(team * PEERS + m),
            device_id_type=MESH,
        )
        copy.start()
        a_copies.append(copy)

    puts = []

    def write(src, dst):
        copy = pltpu.make_async_copy(src, dst, put.at[len(puts)])
        copy.start()
        puts.append(copy)

    def finish_out(g):
        own = pl.ds((g + 1) * half, half)
        both = dot(fc[own, :], wf[0]) + dot(tc[own, :], wf[1])
        both = both + dot(side_by_side(hop(g, tc)), wf[2])
        here = pl.ds(g * half, half)
        out_v[here, :] = both[:, :width] + both[:, width:] + bias
        write(out_v.at[here], out_hbm.at[here])

    def finish_grad(g, arrived):
        here = pl.ds(g * half, half)
        second = back_hop(g + 1, uc)
        if arrived is not None:
            second = second + arrived
        both = dot(wb[0], cc[:, here]) + dot(wb[1], uc[:, here]) + dot(wb[2], stacked(second))
        ig_v[here, :] = (both[:width] + both[width:]).T
        write(ig_v.at[here], ig_hbm.at[here])

    middle = list(range(1, groups - 1))
    for g in middle:
        finish_out(g)

    for copy in a_copies:
        copy.wait_recv()
    summed = grads[rank]
    for o in range(PEERS - 1):
        summed = summed + part_in[o]
    seg[...] = summed
    cross[team] = summed
    b_copies = []
    for o, t in enumerate(others):
        copy = pltpu.make_async_remote_copy(
            src_ref=seg,
            dst_ref=cross.at[team],
            send_sem=b_send.at[o],
            recv_sem=b_recv.at[o],
            device_id=at(t * PEERS + rank),
            device_id_type=MESH,
        )
        copy.start()
        b_copies.append(copy)

    for g in middle:
        finish_grad(g, None)
    for copy in t_swap:
        copy.wait_recv()
    tc[pl.ds(0, half), :] = side_by_side(t_in[0])
    tc[pl.ds(half + rows, half), :] = side_by_side(t_in[1])
    finish_out(0)

    for copy in b_copies:
        copy.wait_recv()
    summed = cross[0]
    for t in range(1, teams):
        summed = summed + cross[t]
    summed = summed * scale
    final[rank] = summed
    for copy in b_copies:
        copy.wait_send()
    seg[...] = summed
    c_copies = []
    for o, m in enumerate(mates):
        copy = pltpu.make_async_remote_copy(
            src_ref=seg,
            dst_ref=final.at[rank],
            send_sem=c_send.at[o],
            recv_sem=c_recv.at[o],
            device_id=at(team * PEERS + m),
            device_id_type=MESH,
        )
        copy.start()
        c_copies.append(copy)

    finish_out(groups - 1)
    for copy in v_swap:
        copy.wait_recv()
    finish_grad(0, v_in[0])
    finish_grad(groups - 1, v_in[1])

    for copy in c_copies:
        copy.wait_recv()
    for s in range(PEERS):
        piece = final[s]
        start = (s % (PEERS // 2)) * rim
        if s < PEERS // 2:
            wg_ref[0, pl.ds(start, rim), :] = piece[:, :chan]
            wg_ref[1, pl.ds(start, rim), :] = piece[:, chan:]
        else:
            wg_ref[2, pl.ds(start, rim), :] = piece[:, :chan]
    bg_ref[...] = final[PEERS // 2][:1, chan:]
    write(wg_ref, wg_hbm)
    write(bg_ref, bg_hbm)

    for copy in f_swap + u_swap + t_swap + v_swap + a_copies + c_copies:
        copy.wait_send()
    for copy in puts:
        copy.wait()


def store(*refs):
    count = 4
    sources, targets, held = refs[:count], refs[count : 2 * count], refs[2 * count : 3 * count]
    arrived, done = refs[3 * count :]
    ins, outs = [], []
    for src, dst, mid in zip(sources, targets, held):
        parts = 4 if src.shape[0] % 32 == 0 else 1
        size = src.shape[0] // parts
        for p in range(parts):
            here = pl.ds(p * size, size)
            k = len(ins)
            ins.append(pltpu.make_async_copy(src.at[here], mid.at[here], arrived.at[k]))
            outs.append(pltpu.make_async_copy(mid.at[here], dst.at[here], done.at[k]))
            ins[-1].start()
    for first, second in zip(ins, outs):
        first.wait()
        second.start()
    for copy in outs:
        copy.wait()


def shards(features, lap_tiles, columns, weights, bias_term, cotangent):
    rows, width = features.shape
    blocks, nb, tile = lap_tiles.shape
    pb = math.isqrt(tile)
    hb = 4
    half = hb * pb
    chan = width // 2
    devices = lax.axis_size("patch") * lax.axis_size("strip")
    teams = devices // PEERS
    rim = 2 * chan // PEERS
    scale = 1.0 / math.sqrt(2 * rows * devices)
    hbm = pl.BlockSpec(memory_space=pltpu.HBM)
    dma = pltpu.SemaphoreType.DMA
    out_shape = (
        jax.ShapeDtypeStruct((rows, width), f32),
        jax.ShapeDtypeStruct((rows, width), f32),
        jax.ShapeDtypeStruct((3, chan, chan), f32),
        jax.ShapeDtypeStruct((1, chan), f32),
    )
    results = pl.pallas_call(
        functools.partial(body, (nb, pb, blocks, hb, blocks * devices, scale)),
        out_shape=out_shape,
        in_specs=[hbm] * 6,
        out_specs=(hbm,) * 4,
        scratch_shapes=[
            pltpu.VMEM((rows, width), f32),
            pltpu.VMEM((rows, width), f32),
            pltpu.VMEM((nb, blocks, tile), f32),
            pltpu.SMEM((nb, blocks), jnp.int32),
            pltpu.VMEM((3, chan, chan), f32),
            pltpu.VMEM((1, chan), f32),
            pltpu.VMEM((blocks * (nb * pb // 2 + 8), 128), f32),
            pltpu.VMEM((2 * rows, 3 * half), bf16),
            pltpu.VMEM((rows + 2 * half, 2 * width), bf16),
            pltpu.VMEM((rows + 2 * half, 2 * width), bf16),
            pltpu.VMEM((2 * width, rows), bf16),
            pltpu.VMEM((2 * width, rows), bf16),
            pltpu.VMEM((3, 2 * width, 2 * width), bf16),
            pltpu.VMEM((3, 2 * width, 2 * width), bf16),
            pltpu.VMEM((rows, width), f32),
            pltpu.VMEM((rows, width), f32),
            pltpu.VMEM((3, chan, chan), f32),
            pltpu.VMEM((1, chan), f32),
            pltpu.VMEM((2, half, width), f32),
            pltpu.VMEM((2, half, width), f32),
            pltpu.VMEM((2, width, half), f32),
            pltpu.VMEM((2, width, half), f32),
            pltpu.VMEM((2, half, width), f32),
            pltpu.VMEM((2, width, half), f32),
            pltpu.VMEM((2, width, half), f32),
            pltpu.VMEM((PEERS, rim, width), f32),
            pltpu.VMEM((PEERS - 1, rim, width), f32),
            pltpu.VMEM((rim, width), f32),
            pltpu.VMEM((teams, rim, width), f32),
            pltpu.VMEM((PEERS, rim, width), f32),
            dma((8,)),
            dma((8,)),
            dma((PEERS - 1,)),
            dma((PEERS - 1,)),
            dma((teams - 1,)),
            dma((teams - 1,)),
            dma((PEERS - 1,)),
            dma((PEERS - 1,)),
            dma((5,)),
            dma((nb,)),
            dma((2 * (blocks // hb) + 2,)),
        ],
        compiler_params=pltpu.CompilerParams(
            collective_id=0, has_side_effects=True, vmem_limit_bytes=62 * 1024 * 1024
        ),
        name="chebyshev",
    )(
        features,
        jnp.transpose(lap_tiles, (1, 0, 2)),
        columns.T,
        weights,
        bias_term.reshape(1, chan),
        cotangent,
    )
    output, input_grad, weight_grad, bias_grad = pl.pallas_call(
        store,
        out_shape=out_shape,
        in_specs=[hbm] * 4,
        out_specs=(hbm,) * 4,
        scratch_shapes=[pltpu.VMEM(leaf.shape, f32) for leaf in out_shape] + [dma((10,))] * 2,
        compiler_params=pltpu.CompilerParams(vmem_limit_bytes=62 * 1024 * 1024),
        name="store",
    )(*results)
    return output, input_grad, weight_grad, bias_grad.reshape(chan)


def solution(mesh):
    split = ("patch", "strip")
    in_specs = (P(split, None), P(split, None, None), P(split, None), P(), P(), P(split, None))
    out_specs = (P(split, None), P(split, None), P(), P())
    return jax.shard_map(shards, mesh=mesh, in_specs=in_specs, out_specs=out_specs, check_vma=False)
```
